512 devices in a mesh: graph: 128 (over z, x, core), dp: 4 (over y).
Axes of the slice: x: 4, y: 4, z: 16, core: 2. Of those that a mesh axis runs over, the one named last changes fastest.
Arguments:
- atoms: bfloat16 [8192, 256], P(('dp', 'graph')), parts along dimension 0, may hold values from -6 to 6
- fetch_rows: int32 [512, 128, 4], P(('dp', 'graph')), parts along dimension 0, may hold values from 0 to 15
- edge_slots: int32 [2, 131072], P(None, ('dp', 'graph')), parts along dimension 1, may hold values from 0 to 511, as said below
- messages: bfloat16 [131072, 1024], P(('dp', 'graph')), parts along dimension 0, may hold values from -6 to 6
- radial: bfloat16 [16, 131072], P(None, ('dp', 'graph')), parts along dimension 1, may hold values from -6 to 6
- angular: bfloat16 [16, 1048576], P(None, ('dp', 'graph')), parts along dimension 1, may hold values from -6 to 6
- trip_edges: int32 [2, 1048576], P(None, ('dp', 'graph')), parts along dimension 1, may hold values from 0 to 255
- trip_blocks: int32 [512], P(('dp', 'graph')), parts along dimension 0, may hold values from 1 to 8, as said below
- reverse_slot: int32 [131072], P(('dp', 'graph')), parts along dimension 0, may hold values from 0 to 255, as said below
- message_weight: bfloat16 [1024, 1024], replicated, may hold values from -0.1875 to 0.1875
- source_weight: bfloat16 [256, 1024], replicated, may hold values from -0.375 to 0.375
- target_weight: bfloat16 [256, 1024], replicated, may hold values from -0.375 to 0.375
- radial_weight: bfloat16 [16, 1024], replicated, may hold values from -1.5 to 1.5
- down_weight: bfloat16 [1024, 128], replicated, may hold values from -0.1875 to 0.1875
- angle_weight: bfloat16 [16, 128], replicated, may hold values from -1.5 to 1.5
- up_ca_weight: bfloat16 [128, 1024], replicated, may hold values from -0.5 to 0.5
- up_ac_weight: bfloat16 [128, 1024], replicated, may hold values from -0.5 to 0.5
Outputs:
- updated: bfloat16 [131072, 1024], P(('dp', 'graph')), parts along dimension 0
- message_grad: bfloat16 [131072, 1024], P(('dp', 'graph')), parts along dimension 0
- atom_grad: float32 [8192, 256], P(('dp', 'graph')), parts along dimension 0
The draws below stay inside these ranges and needn't reach their ends.
There are 4 independent parts, one for each index of `dp`. The reference program is written for one: setup_inputs(seed, part) draws one part's arguments, and reference() takes and returns one part's arrays. A program takes and returns all parts, laid end to end along the dimension named above; an argument that names none is the same for every part. Nothing has to cross between parts.
Inputs may be any that keep to these rules, and one draw needn't show every extreme that they name: `edge_slots`: on each device the 512 slot numbers of its edges use every slot once. `trip_blocks`: triplet slots past the live blocks of a device are padding; some device has all its blocks live. `reverse_slot`: the reverse of an edge on device r lies on device r XOR 1 at the given position, and the reverse of the reverse is the edge itself.
All inputs are finite; a program needn't handle non-finite values.
Results may differ from the reference program's by a relative error of at most 0.0095.
Values may be sent and summed in bfloat16 or wider, within the bound.
A program may use at most 64 MiB of HBM per device.

```python
import jax
import jax.numpy as jnp

EW = 1024
AW = 256
TW = 128
NRAD = 16
NCBF = 16
TBLK = 256
E_DEV = 256
A_DEV = 16
EDGES = 32768
TRIP_DEV = 2048
TRIPS = 262144
ATOMS = 2048
SLOTS_PEER = 4
N_GRAPH = 128


def draw_edge_slots(key, part):
    key = jax.random.fold_in(key, 11)
    groups = EDGES // E_DEV
    keys = jax.random.split(key, groups)

    def one_order(sub_key):
        return jax.random.permutation(sub_key, 2 * E_DEV)
    orders = jax.vmap(one_order)(keys).astype(jnp.int32)
    return orders.reshape(groups, 2, E_DEV).transpose(1, 0, 2).reshape(2, EDGES)


def draw_trip_blocks(key, part):
    key = jax.random.fold_in(key, 12)
    groups = EDGES // E_DEV
    count_key, pick_key = jax.random.split(key)
    counts = jax.random.randint(count_key, (groups,), 1, 4, dtype=jnp.int32)
    chosen = jax.random.randint(pick_key, (), 0, groups, dtype=jnp.int32)
    most = TRIP_DEV // TBLK
    places = jnp.arange(groups, dtype=jnp.int32)
    return jnp.where(places == chosen, most, counts).astype(jnp.int32)


def draw_reverse_slot(key, part):
    key = jax.random.fold_in(key, 13)
    pairs = EDGES // E_DEV // 2
    keys = jax.random.split(key, pairs)

    def one_order(sub_key):
        return jax.random.permutation(sub_key, E_DEV)
    forward = jax.vmap(one_order)(keys).astype(jnp.int32)
    backward = jnp.argsort(forward, axis=1).astype(jnp.int32)
    return jnp.stack([forward, backward], axis=1).reshape(EDGES)


def plant(result, own_key, low, top_value):
    dims = result.shape
    spot = [jax.random.randint(jax.random.fold_in(own_key, axis), (), 0, dims[axis]) for axis in range(len(dims))]
    result = result.at[tuple(spot)].set(low)
    longest = dims.index(max(dims))
    spot[longest] = (spot[longest] + 1) % dims[longest]
    return result.at[tuple(spot)].set(top_value)


def shard_levels(key, shape, cuts, low, top_value):
    level, own = 1.0, jax.random.fold_in(key, 6)
    for axis_at, blocks in cuts:
        heights = jnp.exp(jax.random.uniform(jax.random.fold_in(own, axis_at), (blocks,), jnp.float32, low / len(cuts), top_value / len(cuts)))
        level = level * jnp.repeat(heights, shape[axis_at] // blocks).reshape([-1 if axis == axis_at else 1 for axis in range(len(shape))])
    return level


def noise(key, dims, spread, bound, shards=(), kind=jnp.bfloat16):
    values = spread * jax.random.normal(key, dims, jnp.float32)
    if shards:
        values = values * shard_levels(key, dims, shards, -0.22, 0.18)
    return jnp.clip(values, -bound, bound).astype(kind)


def setup_inputs(seed: int = 0, part: int = 0) -> dict:
    key_list = jax.random.split(jax.random.key(seed), 18)
    part_keys = jax.random.split(jax.random.fold_in(key_list[17], part), 18)
    return {
        "atoms": noise(part_keys[0], (ATOMS, AW), 1.0, 6.0, ((0, 128),)),
        "fetch_rows": plant(jax.random.randint(part_keys[1], (N_GRAPH, N_GRAPH, SLOTS_PEER), 0, A_DEV), jax.random.fold_in(part_keys[1], 1), 0, A_DEV - 1).astype(jnp.int32),
        "edge_slots": draw_edge_slots(jax.random.fold_in(jax.random.fold_in(key_list[17], part), 71), part),
        "messages": noise(part_keys[3], (EDGES, EW), 1.0, 6.0, ((0, 128),)),
        "radial": noise(part_keys[4], (NRAD, EDGES), 1.0, 6.0, ((1, 128),)),
        "angular": noise(part_keys[5], (NCBF, TRIPS), 1.0, 6.0, ((1, 128),)),
        "trip_edges": plant(jax.random.randint(part_keys[6], (2, TRIPS), 0, E_DEV), jax.random.fold_in(part_keys[6], 1), 0, E_DEV - 1).astype(jnp.int32),
        "trip_blocks": draw_trip_blocks(jax.random.fold_in(jax.random.fold_in(key_list[17], part), 71), part),
        "reverse_slot": draw_reverse_slot(jax.random.fold_in(jax.random.fold_in(key_list[17], part), 71), part),
        "message_weight": noise(key_list[9], (EW, EW), EW ** -0.5, 0.1875),
        "source_weight": noise(key_list[10], (AW, EW), AW ** -0.5, 0.375),
        "target_weight": noise(key_list[11], (AW, EW), AW ** -0.5, 0.375),
        "radial_weight": noise(key_list[12], (NRAD, EW), NRAD ** -0.5, 1.5),
        "down_weight": noise(key_list[13], (EW, TW), EW ** -0.5, 0.1875),
        "angle_weight": noise(key_list[14], (NCBF, TW), NCBF ** -0.5, 1.5),
        "up_ca_weight": noise(key_list[15], (TW, EW), TW ** -0.5, 0.5),
        "up_ac_weight": noise(key_list[16], (TW, EW), TW ** -0.5, 0.5),
    }


def silu_grad(values):
    sigma = jax.nn.sigmoid(values)
    return sigma * (1.0 + values * (1.0 - sigma))

def reference(atoms, fetch_rows, edge_slots, messages, radial, angular, trip_edges, trip_blocks, reverse_slot, message_weight, source_weight, target_weight, radial_weight, down_weight, angle_weight, up_ca_weight, up_ac_weight):
    per_peer = fetch_rows.shape[2]
    owners = jnp.arange(N_GRAPH, dtype=jnp.int32)[None, :, None]
    slot_ids = (owners * A_DEV + fetch_rows).reshape(N_GRAPH, N_GRAPH * per_peer)
    edge_dev = jnp.arange(EDGES, dtype=jnp.int32) // E_DEV
    source_id = slot_ids[edge_dev, edge_slots[0]]
    target_id = slot_ids[edge_dev, edge_slots[1]]
    pre = jnp.dot(messages, message_weight, preferred_element_type=jnp.float32)
    pre = pre + jnp.dot(atoms[source_id], source_weight, preferred_element_type=jnp.float32)
    pre = pre + jnp.dot(atoms[target_id], target_weight, preferred_element_type=jnp.float32)
    gate = jnp.dot(radial.T, radial_weight, preferred_element_type=jnp.float32)
    edge_hidden = (jax.nn.silu(pre) * gate).astype(jnp.bfloat16)
    down = jnp.dot(edge_hidden, down_weight, preferred_element_type=jnp.float32)
    reduced = jax.nn.silu(down).astype(jnp.bfloat16)
    basis = jnp.dot(angular.T, angle_weight, preferred_element_type=jnp.float32)
    trip_index = jnp.arange(TRIPS, dtype=jnp.int32)
    trip_dev = trip_index // TRIP_DEV
    live = (trip_index - trip_dev * TRIP_DEV < trip_blocks[trip_dev] * TBLK).astype(jnp.float32)[:, None]
    trip_target = trip_dev * E_DEV + trip_edges[0]
    trip_source = trip_dev * E_DEV + trip_edges[1]
    live_basis = basis * live
    terms = live_basis * reduced[trip_source].astype(jnp.float32)
    gathered = jax.ops.segment_sum(terms, trip_target, num_segments=EDGES).astype(jnp.bfloat16)
    raised_ca = jnp.dot(gathered, up_ca_weight, preferred_element_type=jnp.float32).astype(jnp.bfloat16)
    raised_ac = jnp.dot(gathered, up_ac_weight, preferred_element_type=jnp.float32).astype(jnp.bfloat16)
    reverse = (edge_dev ^ 1) * E_DEV + reverse_slot
    updated = (raised_ca.astype(jnp.float32) + raised_ac[reverse].astype(jnp.float32)).astype(jnp.bfloat16)
    lowered_ca = jnp.dot(updated, up_ca_weight.T, preferred_element_type=jnp.float32)
    lowered_ac = jnp.dot(updated, up_ac_weight.T, preferred_element_type=jnp.float32)
    lowered_grad = lowered_ca + lowered_ac[reverse]
    back_terms = live_basis * lowered_grad[trip_target]
    reduced_grad = jax.ops.segment_sum(back_terms, trip_source, num_segments=EDGES)
    down_grad = (reduced_grad * silu_grad(down)).astype(jnp.bfloat16)
    hidden_grad = jnp.dot(down_grad, down_weight.T, preferred_element_type=jnp.float32)
    pre_grad = (hidden_grad * gate * silu_grad(pre)).astype(jnp.bfloat16)
    message_grad = jnp.dot(pre_grad, message_weight.T, preferred_element_type=jnp.float32).astype(jnp.bfloat16)
    source_grad = jnp.dot(pre_grad, source_weight.T, preferred_element_type=jnp.float32)
    target_grad = jnp.dot(pre_grad, target_weight.T, preferred_element_type=jnp.float32)
    atom_grad = jax.ops.segment_sum(source_grad, source_id, num_segments=ATOMS)
    atom_grad = atom_grad + jax.ops.segment_sum(target_grad, target_id, num_segments=ATOMS)
    return (updated, message_grad, atom_grad)
```

```python
import functools

import jax
import jax.numpy as jnp
from jax import lax
from jax.experimental import pallas as pl
from jax.experimental.pallas import tpu as pltpu
from jax.sharding import PartitionSpec as P

TBLK = 256
PLANE = 8
VMEM = 62 * 1024 * 1024
F32 = jnp.float32
BF16 = jnp.bfloat16
MESH = pl.DeviceIdType.MESH


def iota(shape, dim):
    return lax.broadcasted_iota(jnp.int32, shape, dim)


def dot(left, right):
    return jnp.dot(left, right, preferred_element_type=F32)


def dot_nt(left, right):
    return lax.dot_general(left, right, (((1,), (1,)), ((), ())), preferred_element_type=F32)


def hot(mask):
    return jnp.where(mask, 1.0, 0.0).astype(BF16)


def column(row):
    count = row.shape[1]
    tall = jnp.broadcast_to(row.astype(F32), (128, count))
    return jnp.transpose(tall)


def hot_rows(row, width):
    wide = column(row).astype(jnp.int32)
    parts = [hot(wide == iota(wide.shape, 1) + start) for start in range(0, width, 128)]
    return jnp.concatenate(parts, axis=1)


def kernel(
    plane,
    count,
    blocks_ref,
    *refs,
):
    n_in = 16
    hbm = refs[:n_in]
    updated_out, message_out, atom_out = refs[n_in : n_in + 3]
    vm = refs[n_in + 3 : 2 * n_in + 3]
    (
        atoms,
        fetch,
        slots_in,
        trips,
        reverse,
        angular,
        angle_w,
        radial,
        radial_w,
        down_w,
        up_ca,
        messages,
        message_w,
        source_w,
        up_ac,
        target_w,
    ) = vm
    (
        st,
        tt,
        bt,
        gate,
        pre,
        hidden,
        grad,
        down_t,
        mix,
        edge_rows,
        slot_cols,
        rev_cols,
        sel,
        sel_t,
        pair,
        table,
        want_out,
        want_in,
        rows_out,
        rows_in,
        gather_in,
        back_out,
        back_in,
        part_out,
        part_in,
        updated_v,
        message_v,
        atom_v,
        in_sem,
        out_sem,
        atom_send,
        atom_recv,
        want_send,
        want_recv,
        rows_send,
        rows_recv,
        pair_send,
        pair_recv,
        back_send,
        back_recv,
        part_send,
        part_recv,
    ) = refs[2 * n_in + 3 :]
    depth = count // plane
    per_peer = fetch.shape[0]
    local = atoms.shape[0]
    column_atoms = depth * local
    share = depth * per_peer
    edges, width = messages.shape
    trip_count = trips.shape[1]
    tri = down_w.shape[1]

    me = lax.axis_index("graph")
    my_z, my_q = me // plane, me % plane

    def z_peer(step):
        return (my_z + step) % depth

    def q_peer(step):
        return (my_q + step) % plane

    def at(z, q):
        return {"graph": z * plane + q}

    def remote(src, dst, send, recv, where):
        return pltpu.make_async_remote_copy(
            src_ref=src, dst_ref=dst, send_sem=send, recv_sem=recv, device_id=where, device_id_type=MESH
        )

    barrier = pltpu.get_barrier_semaphore()

    @pl.loop(1, depth)
    def _(step):
        pl.semaphore_signal(barrier, inc=1, device_id=at(z_peer(step), my_q), device_id_type=MESH)

    @pl.loop(1, plane)
    def _(step):
        pl.semaphore_signal(barrier, inc=1, device_id=at(my_z, q_peer(step)), device_id_type=MESH)

    loads = [pltpu.make_async_copy(hbm[i], vm[i], in_sem.at[i]) for i in range(n_in)]
    for load in loads:
        load.start()

    pl.semaphore_wait(barrier, depth + plane - 2)

    def atom_copy(step, slot):
        return remote(atoms, table.at[slot], atom_send.at[step], atom_recv.at[slot], at(z_peer(step), my_q))

    loads[0].wait()

    @pl.loop(1, depth)
    def _(step):
        atom_copy(step, my_z).start()

    table[my_z] = atoms[...]

    loads[1].wait()
    flat = jnp.concatenate([fetch[c : c + 1, :] for c in range(per_peer)], axis=1)
    flat = jnp.broadcast_to(flat.astype(F32), (8, per_peer * count)).astype(BF16)
    from_peer = iota((per_peer * count, 128), 0)
    to_lane = iota((per_peer * count, 128), 1)
    lane = iota((8, 128), 1)
    for q in range(plane):
        pick = hot(
            (from_peer // count == to_lane // depth)
            & (from_peer % count == (to_lane % depth) * plane + q)
        )
        ids = dot(flat, pick).astype(jnp.int32) + (lane % depth) * local
        want_out[q] = jnp.where(lane < share, ids, -1)[0:1, :]

    def want_copy(step, slot):
        return remote(
            want_out.at[q_peer(step)], want_in.at[slot], want_send.at[step], want_recv.at[slot], at(my_z, q_peer(step))
        )

    @pl.loop(1, plane)
    def _(step):
        want_copy(step, my_q).start()

    want_in[my_q] = want_out[my_q]

    loads[3].wait()
    live = blocks_ref[0] * TBLK
    chunk = 512

    @pl.loop(0, trip_count // chunk)
    def _(i):
        span = pl.ds(pl.multiple_of(i * chunk, chunk), chunk)
        edge = iota((edges, chunk), 0)
        at_trip = iota((1, chunk), 1) + i * chunk
        targets = jnp.where(at_trip < live, trips[0:1, span], -1)
        tt[:, span] = hot(edge == targets)
        st[:, span] = hot(edge == trips[1:2, span])

    loads[5].wait()
    loads[6].wait()
    bt[...] = dot(jnp.transpose(angle_w[...].astype(F32)).astype(BF16), angular[...])

    loads[2].wait()
    loads[4].wait()
    slot = slots_in[...]
    owner = slot // per_peer
    slot = (owner % plane) * share + (slot % per_peer) * depth + owner // plane
    total = plane * share
    for role in range(2):
        row = slot[role : role + 1, :]
        edge_rows[role] = hot_rows(row, total)
        slot_cols[:, role * edges : (role + 1) * edges] = hot(iota((total, edges), 0) == row)
    rev_cols[...] = hot(iota((edges, edges), 0) == reverse[...])

    def want_wait(step):
        want_copy(step, q_peer(step)).wait_recv()

    @pl.loop(1, plane)
    def _(step):
        want_wait(step)

    for q in range(plane):
        sel[q * share : (q + 1) * share, :] = hot_rows(want_in[q], column_atoms)[:share]

    loads[9].wait()
    down_t[...] = jnp.transpose(down_w[...].astype(F32)).astype(BF16)

    @pl.loop(1, depth)
    def _(step):
        atom_copy(step, z_peer(step)).wait_recv()

    rows = dot(sel[...], table[...].reshape(column_atoms, atoms.shape[1])).astype(BF16)
    rows_out[...] = rows.reshape(rows_out.shape)

    def rows_copy(step, slot_at):
        return remote(
            rows_out.at[q_peer(step)], rows_in.at[slot_at], rows_send.at[step], rows_recv.at[slot_at], at(my_z, q_peer(step))
        )

    @pl.loop(1, plane)
    def _(step):
        rows_copy(step, my_q).start()

    rows_in[my_q] = rows_out[my_q]

    sel_t[...] = jnp.transpose(sel[...].astype(F32)).astype(BF16)
    loads[7].wait()
    loads[8].wait()
    gate[...] = dot(jnp.transpose(radial[...].astype(F32)).astype(BF16), radial_w[...])
    loads[10].wait()
    loads[14].wait()
    same = dot_nt(up_ca[...], up_ca[...]) + dot_nt(up_ac[...], up_ac[...])
    cross = dot_nt(up_ac[...], up_ca[...])
    cross = cross + jnp.transpose(cross)
    both = jnp.concatenate([same, cross], axis=1)
    high = both.astype(BF16)
    mix[:tri, :] = high
    mix[tri:, :] = (both - high.astype(F32)).astype(BF16)
    loads[11].wait()
    loads[12].wait()
    tile = 256

    @pl.loop(0, width // tile)
    def _(i):
        span = pl.ds(pl.multiple_of(i * tile, tile), tile)
        pre[:, span] = dot(messages[...], message_w[:, span])

    loads[13].wait()
    loads[15].wait()

    @pl.loop(1, plane)
    def _(step):
        rows_copy(step, q_peer(step)).wait_recv()

    slot_rows = rows_in[...].reshape(total, atoms.shape[1])
    source_rows = dot(edge_rows[0], slot_rows).astype(BF16)
    target_rows = dot(edge_rows[1], slot_rows).astype(BF16)
    down = jnp.zeros((tri, edges), F32)
    for start in range(0, width, tile):
        span = slice(start, start + tile)
        part = pre[:, span] + dot(source_rows, source_w[:, span]) + dot(target_rows, target_w[:, span])
        pre[:, span] = part
        hidden[:, span] = (part * jax.nn.sigmoid(part) * gate[:, span]).astype(BF16)
        down = down + dot_nt(down_t[:, span], hidden[:, span])
    reduced = (down * jax.nn.sigmoid(down)).astype(BF16)
    terms = (dot(reduced, st[...]) * bt[...]).astype(BF16)
    gathered = dot_nt(terms, tt[...]).astype(BF16)
    pair[:tri, :] = gathered

    pair_copy = remote(
        pair.at[pl.ds(0, tri)], gather_in, pair_send, pair_recv, at(my_z, my_q + 1 - 2 * (my_q % 2))
    )
    pair_copy.start()

    sigma = jax.nn.sigmoid(down)
    down_slope = sigma * (1.0 + down * (1.0 - sigma))
    for start in range(0, width, tile):
        span = slice(start, start + tile)
        part = pre[:, span]
        sigma = jax.nn.sigmoid(part)
        gate[:, span] = gate[:, span] * (sigma * (1.0 + part * (1.0 - sigma)))

    pair_copy.wait_recv()
    pair[tri:, :] = dot(gather_in[...], rev_cols[...]).astype(BF16)
    lowered = dot(mix[...], pair[...])
    lowered = (lowered[:tri] + lowered[tri:]).astype(BF16)

    terms = (dot(lowered, tt[...]) * bt[...]).astype(BF16)
    down_grad = dot_nt(terms, st[...]) * down_slope
    down_grad = jnp.transpose(down_grad).astype(BF16)
    ends = [jnp.zeros((edges, atoms.shape[1]), F32) for _ in range(2)]
    for start in range(0, width, tile):
        span = slice(start, start + tile)
        part = (dot(down_grad, down_t[:, span]) * gate[:, span]).astype(BF16)
        grad[:, span] = part
        ends[0] = ends[0] + dot_nt(part, source_w[:, span])
        ends[1] = ends[1] + dot_nt(part, target_w[:, span])
    ends = jnp.concatenate([ends[0].astype(BF16), ends[1].astype(BF16)], axis=0)
    back_out[...] = dot(slot_cols[...], ends).astype(BF16).reshape(back_out.shape)

    def back_copy(step, slot_at):
        return remote(
            back_out.at[q_peer(step)], back_in.at[slot_at], back_send.at[step], back_recv.at[slot_at], at(my_z, q_peer(step))
        )

    @pl.loop(1, plane)
    def _(step):
        back_copy(step, my_q).start()

    back_in[my_q] = back_out[my_q]

    mixed = jnp.transpose(pair[...].astype(F32)).astype(BF16)
    for start in range(0, width, tile):
        span = slice(start, start + tile)
        raised = dot(mixed[:, :tri], up_ca[:, span]) + dot(mixed[:, tri:], up_ac[:, span])
        updated_v[:, span] = raised.astype(BF16)
    updated_copy = pltpu.make_async_copy(updated_v, updated_out, out_sem.at[0])
    updated_copy.start()

    @pl.loop(1, plane)
    def _(step):
        back_copy(step, q_peer(step)).wait_recv()

    part = dot(sel_t[...], back_in[...].reshape(total, atoms.shape[1]))
    part_out[...] = part.astype(BF16).reshape(part_out.shape)

    def part_copy(step, slot_at):
        return remote(
            part_out.at[z_peer(step)], part_in.at[slot_at], part_send.at[step], part_recv.at[slot_at], at(z_peer(step), my_q)
        )

    @pl.loop(1, depth)
    def _(step):
        part_copy(step, my_z).start()

    part_in[my_z] = part_out[my_z]

    @pl.loop(0, width // tile)
    def _(i):
        span = pl.ds(pl.multiple_of(i * tile, tile), tile)
        message_v[:, span] = dot_nt(grad[...], message_w[span, :]).astype(BF16)

    message_copy = pltpu.make_async_copy(message_v, message_out, out_sem.at[1])
    message_copy.start()

    @pl.loop(1, depth)
    def _(step):
        part_copy(step, z_peer(step)).wait_recv()

    owned = part_in[0].astype(F32)
    for z in range(1, depth):
        owned = owned + part_in[z].astype(F32)
    atom_v[...] = owned
    atom_copy_out = pltpu.make_async_copy(atom_v, atom_out, out_sem.at[2])
    atom_copy_out.start()

    @pl.loop(1, depth)
    def _(step):
        atom_copy(step, my_z).wait_send()
        part_copy(step, my_z).wait_send()

    @pl.loop(1, plane)
    def _(step):
        want_copy(step, my_q).wait_send()
        rows_copy(step, my_q).wait_send()
        back_copy(step, my_q).wait_send()

    pair_copy.wait_send()
    updated_copy.wait()
    message_copy.wait()
    atom_copy_out.wait()


def shards(
    atoms,
    fetch_rows,
    edge_slots,
    messages,
    radial,
    angular,
    trip_edges,
    trip_blocks,
    reverse_slot,
    message_weight,
    source_weight,
    target_weight,
    radial_weight,
    down_weight,
    angle_weight,
    up_ca_weight,
    up_ac_weight,
):
    count = lax.axis_size("graph")
    plane = PLANE
    depth = count // plane
    local, atom_width = atoms.shape
    edges, width = messages.shape
    tri = down_weight.shape[1]
    trip_count = trip_edges.shape[1]
    per_peer = fetch_rows.shape[2]
    share = depth * per_peer
    total = plane * share
    fetch = jnp.transpose(fetch_rows[0])
    operands = (
        atoms,
        fetch,
        edge_slots,
        trip_edges,
        reverse_slot.reshape(1, edges),
        angular,
        angle_weight,
        radial,
        radial_weight,
        down_weight,
        up_ca_weight,
        messages,
        message_weight,
        source_weight,
        up_ac_weight,
        target_weight,
    )
    V = pltpu.VMEM
    DMA = pltpu.SemaphoreType.DMA
    scratch = [V(x.shape, x.dtype) for x in operands] + [
        V((edges, trip_count), BF16),
        V((edges, trip_count), BF16),
        V((tri, trip_count), F32),
        V((edges, width), F32),
        V((edges, width), F32),
        V((edges, width), BF16),
        V((edges, width), BF16),
        V((tri, width), BF16),
        V((2 * tri, 2 * tri), BF16),
        V((2, edges, total), BF16),
        V((total, 2 * edges), BF16),
        V((edges, edges), BF16),
        V((total, depth * local), BF16),
        V((depth * local, total), BF16),
        V((2 * tri, edges), BF16),
        V((depth, local, atom_width), BF16),
        V((plane, 1, 128), jnp.int32),
        V((plane, 1, 128), jnp.int32),
        V((plane, share, atom_width), BF16),
        V((plane, share, atom_width), BF16),
        V((tri, edges), BF16),
        V((plane, share, atom_width), BF16),
        V((plane, share, atom_width), BF16),
        V((depth, local, atom_width), BF16),
        V((depth, local, atom_width), BF16),
        V((edges, width), BF16),
        V((edges, width), BF16),
        V((local, atom_width), F32),
        DMA((16,)),
        DMA((3,)),
        DMA((depth,)),
        DMA((depth,)),
        DMA((plane,)),
        DMA((plane,)),
        DMA((plane,)),
        DMA((plane,)),
        DMA,
        DMA,
        DMA((plane,)),
        DMA((plane,)),
        DMA((depth,)),
        DMA((depth,)),
    ]
    return pl.pallas_call(
        functools.partial(kernel, plane, count),
        out_shape=(
            jax.ShapeDtypeStruct((edges, width), BF16),
            jax.ShapeDtypeStruct((edges, width), BF16),
            jax.ShapeDtypeStruct((local, atom_width), F32),
        ),
        in_specs=[pl.BlockSpec(memory_space=pltpu.SMEM)] + [pl.BlockSpec(memory_space=pl.ANY)] * len(operands),
        out_specs=[pl.BlockSpec(memory_space=pl.ANY)] * 3,
        scratch_shapes=scratch,
        compiler_params=pltpu.CompilerParams(
            collective_id=0, has_side_effects=True, vmem_limit_bytes=VMEM
        ),
        cost_estimate=pl.CostEstimate(flops=3_000_000_000, bytes_accessed=8_000_000, transcendentals=1_000_000),
    )(trip_blocks, *operands)


def solution(mesh):
    both = ("dp", "graph")
    rows, lanes = P(both, None), P(None, both)
    placed = (
        rows,
        P(both, None, None),
        lanes,
        rows,
        lanes,
        lanes,
        lanes,
        P(both),
        P(both),
    ) + (P(),) * 8
    return jax.shard_map(
        shards,
        mesh=mesh,
        in_specs=placed,
        out_specs=(rows, rows, rows),
        check_vma=False,
    )
```

```python
import functools

import jax
import jax.numpy as jnp
from jax import lax
from jax.experimental import pallas as pl
from jax.experimental.pallas import tpu as pltpu
from jax.sharding import PartitionSpec as P

TBLK = 256
PLANE = 8
VMEM = 56 * 1024 * 1024
F32 = jnp.float32
BF16 = jnp.bfloat16
MESH = pl.DeviceIdType.MESH


def iota(shape, dim):
    return lax.broadcasted_iota(jnp.int32, shape, dim)


def dot(left, right):
    return jnp.dot(left, right, preferred_element_type=F32)


def dot_nt(left, right):
    return lax.dot_general(left, right, (((1,), (1,)), ((), ())), preferred_element_type=F32)


def hot(mask):
    return jnp.where(mask, 1.0, 0.0).astype(BF16)


def column(row):
    count = row.shape[1]
    tall = jnp.broadcast_to(row.astype(F32), (128, count))
    return jnp.transpose(tall)


def hot_rows(row, width):
    wide = column(row).astype(jnp.int32)
    parts = [hot(wide == iota(wide.shape, 1) + start) for start in range(0, width, 128)]
    return jnp.concatenate(parts, axis=1)


def kernel(
    plane,
    count,
    *refs,
):
    n_in = 16
    blocks_hbm, *hbm = refs[: n_in + 1]
    updated_out, message_out, atom_out = refs[n_in + 1 : n_in + 4]
    vm = refs[n_in + 4 : 2 * n_in + 4]
    (
        atoms,
        fetch,
        slots_in,
        trips,
        reverse,
        angular,
        angle_w,
        radial,
        radial_w,
        down_w,
        up_ca,
        messages,
        message_w,
        source_w,
        up_ac,
        target_w,
    ) = vm
    (
        st,
        tt,
        bt,
        gate,
        pre,
        hidden,
        grad,
        down_t,
        mix,
        edge_rows,
        slot_cols,
        rev_cols,
        sel,
        sel_t,
        pair,
        table,
        want_out,
        want_in,
        rows_out,
        rows_in,
        gather_in,
        back_out,
        back_in,
        part_out,
        part_in,
        blocks,
        in_sem,
        atom_send,
        atom_recv,
        want_send,
        want_recv,
        rows_send,
        rows_recv,
        pair_send,
        pair_recv,
        back_send,
        back_recv,
        part_send,
        part_recv,
    ) = refs[2 * n_in + 4 :]
    depth = count // plane
    per_peer = fetch.shape[0]
    local = atoms.shape[0]
    column_atoms = depth * local
    share = depth * per_peer
    edges, width = messages.shape
    trip_count = trips.shape[1]
    tri = down_w.shape[1]

    me = lax.axis_index("graph")
    my_z, my_q = me // plane, me % plane

    def far_first(step, size):
        return size // 2 + (step // 2) * (2 * (step % 2) - 1)

    def z_peer(step):
        return (my_z + far_first(step, depth)) % depth

    def q_peer(step):
        return (my_q + far_first(step, plane)) % plane

    def at(z, q):
        return {"graph": z * plane + q}

    def remote(src, dst, send, recv, where):
        return pltpu.make_async_remote_copy(
            src_ref=src, dst_ref=dst, send_sem=send, recv_sem=recv, device_id=where, device_id_type=MESH
        )

    barrier = pltpu.get_barrier_semaphore()

    @pl.loop(1, depth)
    def _(step):
        pl.semaphore_signal(barrier, inc=1, device_id=at(z_peer(step), my_q), device_id_type=MESH)

    @pl.loop(1, plane)
    def _(step):
        pl.semaphore_signal(barrier, inc=1, device_id=at(my_z, q_peer(step)), device_id_type=MESH)

    loads = [pltpu.make_async_copy(hbm[i], vm[i], in_sem.at[i]) for i in range(n_in)]
    loads.append(pltpu.make_async_copy(blocks_hbm, blocks, in_sem.at[n_in]))
    for load in loads:
        load.start()

    pl.semaphore_wait(barrier, depth + plane - 2)

    def atom_copy(step, slot):
        return remote(atoms, table.at[slot], atom_send.at[step], atom_recv.at[slot], at(z_peer(step), my_q))

    loads[0].wait()

    @pl.loop(1, depth)
    def _(step):
        atom_copy(step, my_z).start()

    table[my_z] = atoms[...]

    loads[1].wait()
    flat = jnp.concatenate([fetch[c : c + 1, :] for c in range(per_peer)], axis=1)
    flat = jnp.broadcast_to(flat.astype(F32), (8, per_peer * count)).astype(BF16)
    from_peer = iota((per_peer * count, 128), 0)
    to_lane = iota((per_peer * count, 128), 1)
    lane = iota((8, 128), 1)
    for q in range(plane):
        pick = hot(
            (from_peer // count == to_lane // depth)
            & (from_peer % count == (to_lane % depth) * plane + q)
        )
        ids = dot(flat, pick).astype(jnp.int32) + (lane % depth) * local
        want_out[q] = jnp.where(lane < share, ids, -1)[0:1, :]

    def want_copy(step, slot):
        return remote(
            want_out.at[q_peer(step)], want_in.at[slot], want_send.at[step], want_recv.at[slot], at(my_z, q_peer(step))
        )

    @pl.loop(1, plane)
    def _(step):
        want_copy(step, my_q).start()

    want_in[my_q] = want_out[my_q]

    loads[3].wait()
    loads[n_in].wait()
    live = blocks[...] * TBLK
    chunk = 512

    @pl.loop(0, trip_count // chunk)
    def _(i):
        span = pl.ds(pl.multiple_of(i * chunk, chunk), chunk)
        edge = iota((edges, chunk), 0)
        at_trip = iota((1, chunk), 1) + i * chunk
        targets = jnp.where(at_trip < live, trips[0:1, span], -1)
        tt[:, span] = hot(edge == targets)
        st[:, span] = hot(edge == trips[1:2, span])

    loads[5].wait()
    loads[6].wait()
    bt[...] = dot(jnp.transpose(angle_w[...].astype(F32)).astype(BF16), angular[...])

    loads[2].wait()
    loads[4].wait()
    slot = slots_in[...]
    owner = slot // per_peer
    slot = (owner % plane) * share + (slot % per_peer) * depth + owner // plane
    total = plane * share
    for role in range(2):
        row = slot[role : role + 1, :]
        edge_rows[role] = hot_rows(row, total)
        slot_cols[:, role * edges : (role + 1) * edges] = hot(iota((total, edges), 0) == row)
    rev_cols[...] = hot(iota((edges, edges), 0) == reverse[...])

    def want_wait(step):
        want_copy(step, q_peer(step)).wait_recv()

    @pl.loop(1, plane)
    def _(step):
        want_wait(step)

    for q in range(plane):
        sel[q * share : (q + 1) * share, :] = hot_rows(want_in[q], column_atoms)[:share]

    loads[9].wait()
    down_t[...] = jnp.transpose(down_w[...].astype(F32)).astype(BF16)

    @pl.loop(1, depth)
    def _(step):
        atom_copy(step, z_peer(step)).wait_recv()

    rows = dot(sel[...], table[...].reshape(column_atoms, atoms.shape[1])).astype(BF16)
    rows_out[...] = rows.reshape(rows_out.shape)

    def rows_copy(step, slot_at):
        return remote(
            rows_out.at[q_peer(step)], rows_in.at[slot_at], rows_send.at[step], rows_recv.at[slot_at], at(my_z, q_peer(step))
        )

    @pl.loop(1, plane)
    def _(step):
        rows_copy(step, my_q).start()

    rows_in[my_q] = rows_out[my_q]

    sel_t[...] = jnp.transpose(sel[...].astype(F32)).astype(BF16)
    loads[7].wait()
    loads[8].wait()
    gate[...] = dot(jnp.transpose(radial[...].astype(F32)).astype(BF16), radial_w[...])
    loads[10].wait()
    loads[14].wait()
    same = dot_nt(up_ca[...], up_ca[...]) + dot_nt(up_ac[...], up_ac[...])
    cross = dot_nt(up_ac[...], up_ca[...])
    cross = cross + jnp.transpose(cross)
    both = jnp.concatenate([same, cross], axis=1)
    high = both.astype(BF16)
    mix[:tri, :] = high
    mix[tri:, :] = (both - high.astype(F32)).astype(BF16)
    loads[11].wait()
    loads[12].wait()
    tile = 256

    @pl.loop(0, width // tile)
    def _(i):
        span = pl.ds(pl.multiple_of(i * tile, tile), tile)
        pre[:, span] = dot(messages[...], message_w[:, span])

    loads[13].wait()
    loads[15].wait()

    @pl.loop(1, plane)
    def _(step):
        rows_copy(step, q_peer(step)).wait_recv()

    slot_rows = rows_in[...].reshape(total, atoms.shape[1])
    source_rows = dot(edge_rows[0], slot_rows).astype(BF16)
    target_rows = dot(edge_rows[1], slot_rows).astype(BF16)
    down = jnp.zeros((tri, edges), F32)
    for start in range(0, width, tile):
        span = slice(start, start + tile)
        part = pre[:, span] + dot(source_rows, source_w[:, span]) + dot(target_rows, target_w[:, span])
        pre[:, span] = part
        hidden[:, span] = (part * jax.nn.sigmoid(part) * gate[:, span]).astype(BF16)
        down = down + dot_nt(down_t[:, span], hidden[:, span])
    reduced = (down * jax.nn.sigmoid(down)).astype(BF16)
    terms = (dot(reduced, st[...]) * bt[...]).astype(BF16)
    gathered = dot_nt(terms, tt[...]).astype(BF16)
    pair[:tri, :] = gathered

    pair_copy = remote(
        pair.at[pl.ds(0, tri)], gather_in, pair_send, pair_recv, at(my_z, my_q + 1 - 2 * (my_q % 2))
    )
    pair_copy.start()

    sigma = jax.nn.sigmoid(down)
    down_slope = sigma * (1.0 + down * (1.0 - sigma))
    for start in range(0, width, tile):
        span = slice(start, start + tile)
        part = pre[:, span]
        sigma = jax.nn.sigmoid(part)
        gate[:, span] = gate[:, span] * (sigma * (1.0 + part * (1.0 - sigma)))

    pair_copy.wait_recv()
    pair[tri:, :] = dot(gather_in[...], rev_cols[...]).astype(BF16)
    lowered = dot(mix[...], pair[...])
    lowered = (lowered[:tri] + lowered[tri:]).astype(BF16)

    terms = (dot(lowered, tt[...]) * bt[...]).astype(BF16)
    down_grad = dot_nt(terms, st[...]) * down_slope
    down_grad = jnp.transpose(down_grad).astype(BF16)
    ends = [jnp.zeros((edges, atoms.shape[1]), F32) for _ in range(2)]
    for start in range(0, width, tile):
        span = slice(start, start + tile)
        part = (dot(down_grad, down_t[:, span]) * gate[:, span]).astype(BF16)
        grad[:, span] = part
        ends[0] = ends[0] + dot_nt(part, source_w[:, span])
        ends[1] = ends[1] + dot_nt(part, target_w[:, span])
    ends = jnp.concatenate([ends[0].astype(BF16), ends[1].astype(BF16)], axis=0)
    back_out[...] = dot(slot_cols[...], ends).astype(BF16).reshape(back_out.shape)

    def back_copy(step, slot_at):
        return remote(
            back_out.at[q_peer(step)], back_in.at[slot_at], back_send.at[step], back_recv.at[slot_at], at(my_z, q_peer(step))
        )

    @pl.loop(1, plane)
    def _(step):
        back_copy(step, my_q).start()

    back_in[my_q] = back_out[my_q]

    mixed = jnp.transpose(pair[...].astype(F32)).astype(BF16)
    for start in range(0, width, tile):
        span = slice(start, start + tile)
        raised = dot(mixed[:, :tri], up_ca[:, span]) + dot(mixed[:, tri:], up_ac[:, span])
        updated_out[:, span] = raised.astype(BF16)

    @pl.loop(1, plane)
    def _(step):
        back_copy(step, q_peer(step)).wait_recv()

    part = dot(sel_t[...], back_in[...].reshape(total, atoms.shape[1]))
    part_out[...] = part.astype(BF16).reshape(part_out.shape)

    def part_copy(step, slot_at):
        return remote(
            part_out.at[z_peer(step)], part_in.at[slot_at], part_send.at[step], part_recv.at[slot_at], at(z_peer(step), my_q)
        )

    @pl.loop(1, depth)
    def _(step):
        part_copy(step, my_z).start()

    part_in[my_z] = part_out[my_z]

    @pl.loop(0, width // tile)
    def _(i):
        span = pl.ds(pl.multiple_of(i * tile, tile), tile)
        message_out[:, span] = dot_nt(grad[...], message_w[span, :]).astype(BF16)


    @pl.loop(1, depth)
    def _(step):
        part_copy(step, z_peer(step)).wait_recv()

    owned = part_in[0].astype(F32)
    for z in range(1, depth):
        owned = owned + part_in[z].astype(F32)
    atom_out[...] = owned

    @pl.loop(1, depth)
    def _(step):
        atom_copy(step, my_z).wait_send()
        part_copy(step, my_z).wait_send()

    @pl.loop(1, plane)
    def _(step):
        want_copy(step, my_q).wait_send()
        rows_copy(step, my_q).wait_send()
        back_copy(step, my_q).wait_send()

    pair_copy.wait_send()


def shards(
    atoms,
    fetch_rows,
    edge_slots,
    messages,
    radial,
    angular,
    trip_edges,
    trip_blocks,
    reverse_slot,
    message_weight,
    source_weight,
    target_weight,
    radial_weight,
    down_weight,
    angle_weight,
    up_ca_weight,
    up_ac_weight,
):
    count = lax.axis_size("graph")
    plane = PLANE
    depth = count // plane
    local, atom_width = atoms.shape
    edges, width = messages.shape
    tri = down_weight.shape[1]
    trip_count = trip_edges.shape[1]
    per_peer = fetch_rows.shape[2]
    share = depth * per_peer
    total = plane * share
    fetch = jnp.transpose(fetch_rows[0])
    operands = (
        atoms,
        fetch,
        edge_slots,
        trip_edges,
        reverse_slot.reshape(1, edges),
        angular,
        angle_weight,
        radial,
        radial_weight,
        down_weight,
        up_ca_weight,
        messages,
        message_weight,
        source_weight,
        up_ac_weight,
        target_weight,
    )
    V = pltpu.VMEM
    DMA = pltpu.SemaphoreType.DMA
    scratch = [V(x.shape, x.dtype) for x in operands] + [
        V((edges, trip_count), BF16),
        V((edges, trip_count), BF16),
        V((tri, trip_count), F32),
        V((edges, width), F32),
        V((edges, width), F32),
        V((edges, width), BF16),
        V((edges, width), BF16),
        V((tri, width), BF16),
        V((2 * tri, 2 * tri), BF16),
        V((2, edges, total), BF16),
        V((total, 2 * edges), BF16),
        V((edges, edges), BF16),
        V((total, depth * local), BF16),
        V((depth * local, total), BF16),
        V((2 * tri, edges), BF16),
        V((depth, local, atom_width), BF16),
        V((plane, 1, 128), jnp.int32),
        V((plane, 1, 128), jnp.int32),
        V((plane, share, atom_width), BF16),
        V((plane, share, atom_width), BF16),
        V((tri, edges), BF16),
        V((plane, share, atom_width), BF16),
        V((plane, share, atom_width), BF16),
        V((depth, local, atom_width), BF16),
        V((depth, local, atom_width), BF16),
        V((1, 1), jnp.int32),
        DMA((17,)),
        DMA((depth,)),
        DMA((depth,)),
        DMA((plane,)),
        DMA((plane,)),
        DMA((plane,)),
        DMA((plane,)),
        DMA,
        DMA,
        DMA((plane,)),
        DMA((plane,)),
        DMA((depth,)),
        DMA((depth,)),
    ]
    return pl.pallas_call(
        functools.partial(kernel, plane, count),
        out_shape=(
            pltpu.VMEM((edges, width), BF16),
            pltpu.VMEM((edges, width), BF16),
            pltpu.VMEM((local, atom_width), F32),
        ),
        in_specs=[pl.BlockSpec(memory_space=pl.ANY)] * (1 + len(operands)),
        out_specs=[pl.BlockSpec(memory_space=pltpu.VMEM)] * 3,
        scratch_shapes=scratch,
        compiler_params=pltpu.CompilerParams(
            collective_id=0, has_side_effects=True, vmem_limit_bytes=VMEM
        ),
        cost_estimate=pl.CostEstimate(flops=3_000_000_000, bytes_accessed=8_000_000, transcendentals=1_000_000),
    )(trip_blocks.reshape(1, 1), *operands)


def solution(mesh):
    both = ("dp", "graph")
    rows, lanes = P(both, None), P(None, both)
    placed = (
        rows,
        P(both, None, None),
        lanes,
        rows,
        lanes,
        lanes,
        lanes,
        P(both),
        P(both),
    ) + (P(),) * 8
    return jax.shard_map(
        shards,
        mesh=mesh,
        in_specs=placed,
        out_specs=(rows, rows, rows),
        check_vma=False,
    )
```

```python
import functools

import jax
import jax.numpy as jnp
from jax import lax
from jax.experimental import pallas as pl
from jax.experimental.pallas import tpu as pltpu
from jax.sharding import PartitionSpec as P

TBLK = 256
PLANE = 8
VMEM = 56 * 1024 * 1024
F32 = jnp.float32
BF16 = jnp.bfloat16
MESH = pl.DeviceIdType.MESH


def iota(shape, dim):
    return lax.broadcasted_iota(jnp.int32, shape, dim)


def dot(left, right):
    return jnp.dot(left, right, preferred_element_type=F32)


def dot_nt(left, right):
    return lax.dot_general(left, right, (((1,), (1,)), ((), ())), preferred_element_type=F32)


def hot(mask):
    return jnp.where(mask, 1.0, 0.0).astype(BF16)


def column(row):
    count = row.shape[1]
    tall = jnp.broadcast_to(row.astype(F32), (128, count))
    return jnp.transpose(tall)


def hot_rows(row, width):
    wide = column(row).astype(jnp.int32)
    parts = [hot(wide == iota(wide.shape, 1) + start) for start in range(0, width, 128)]
    return jnp.concatenate(parts, axis=1)


def kernel(
    plane,
    count,
    *refs,
):
    n_in = 16
    blocks_hbm, *hbm = refs[: n_in + 1]
    updated_out, message_out, atom_out = refs[n_in + 1 : n_in + 4]
    vm = refs[n_in + 4 : 2 * n_in + 4]
    (
        atoms,
        fetch,
        slots_in,
        trips,
        reverse,
        angular,
        angle_w,
        radial,
        radial_w,
        down_w,
        up_ca,
        messages,
        message_w,
        source_w,
        up_ac,
        target_w,
    ) = vm
    (
        st,
        tt,
        bt,
        gate,
        pre,
        hidden,
        grad,
        down_t,
        rt,
        y,
        mix,
        edge_rows,
        slot_cols,
        rev_cols,
        sel,
        sel_t,
        gather_out,
        table,
        want_out,
        want_in,
        rows_out,
        rows_in,
        gather_in,
        back_out,
        back_in,
        part_out,
        part_in,
        blocks,
        in_sem,
        atom_send,
        atom_recv,
        want_send,
        want_recv,
        rows_send,
        rows_recv,
        pair_send,
        pair_recv,
        back_send,
        back_recv,
        part_send,
        part_recv,
    ) = refs[2 * n_in + 4 :]
    depth = count // plane
    half = depth // 2
    own = half // 2
    per_peer = fetch.shape[0]
    local, atom_width = atoms.shape
    share = half * per_peer
    total = plane * share
    edges, width = messages.shape
    trip_count = trips.shape[1]
    tri = down_w.shape[1]
    tile = 256

    me = lax.axis_index("graph")
    my_z, my_q = me // plane, me % plane

    def far_first(step, size):
        return size // 2 + (step // 2) * (2 * (step % 2) - 1)

    def z_peer(step):
        return (my_z + far_first(step, depth)) % depth

    def q_peer(step):
        return (my_q + far_first(step, plane)) % plane

    def to_slot(step):
        return (own + far_first(step, depth)) % depth

    def from_slot(step):
        return (own - far_first(step, depth) + depth) % depth

    def at(z, q):
        return {"graph": z * plane + q}

    def remote(src, dst, send, recv, where):
        return pltpu.make_async_remote_copy(
            src_ref=src, dst_ref=dst, send_sem=send, recv_sem=recv, device_id=where, device_id_type=MESH
        )

    barrier = pltpu.get_barrier_semaphore()

    @pl.loop(1, depth)
    def _(step):
        pl.semaphore_signal(barrier, inc=1, device_id=at(z_peer(step), my_q), device_id_type=MESH)

    @pl.loop(1, plane)
    def _(step):
        pl.semaphore_signal(barrier, inc=1, device_id=at(my_z, q_peer(step)), device_id_type=MESH)

    loads = [pltpu.make_async_copy(hbm[i], vm[i], in_sem.at[i]) for i in range(n_in)]
    loads.append(pltpu.make_async_copy(blocks_hbm, blocks, in_sem.at[n_in]))
    for load in [loads[n_in]] + loads[:n_in]:
        load.start()

    loads[1].wait()
    flat = jnp.concatenate([fetch[c : c + 1, :] for c in range(per_peer)], axis=1)
    flat = jnp.broadcast_to(flat.astype(F32), (8, per_peer * count)).astype(BF16)
    from_peer = iota((per_peer * count, 128), 0)
    to_lane = iota((per_peer * count, 128), 1)
    lane_z = (my_z + (to_lane // share) * half + to_lane % half + depth - own) % depth
    lane_c = (to_lane % share) // half
    same_c = from_peer // count == lane_c
    offset = from_peer % count - lane_z * plane
    lane = iota((8, 128), 1)
    for q in range(plane):
        pick = hot(same_c & (offset == q))
        ids = dot(flat, pick).astype(jnp.int32) + (lane % half) * local
        want_out[q] = jnp.where(lane < 2 * share, ids, -1)[0:1, :]

    loads[2].wait()
    slot = slots_in[...]
    owner = slot // per_peer
    place = (owner // plane - my_z + own + depth) % depth
    slot = (place // half) * total + (owner % plane) * share + (slot % per_peer) * half + place % half
    for role in range(2):
        row = slot[role : role + 1, :]
        edge_rows[role] = hot_rows(row, 2 * total)
        slot_cols[:, role * edges : (role + 1) * edges] = hot(iota((2 * total, edges), 0) == row)

    loads[n_in].wait()
    loads[3].wait()
    live = blocks[...] * TBLK
    chunk = 512

    @pl.loop(0, trip_count // chunk)
    def _(i):
        span = pl.ds(pl.multiple_of(i * chunk, chunk), chunk)
        edge = iota((edges, chunk), 0)
        at_trip = iota((1, chunk), 1) + i * chunk
        targets = jnp.where(at_trip < live, trips[0:1, span], -1)
        tt[:, span] = hot(edge == targets)
        st[:, span] = hot(edge == trips[1:2, span])

    loads[0].wait()
    table[own] = atoms[...]

    pl.semaphore_wait(barrier, depth + plane - 2)

    def atom_copy(step, slot_at):
        return remote(atoms, table.at[slot_at], atom_send.at[step], atom_recv.at[slot_at], at(z_peer(step), my_q))

    @pl.loop(1, depth)
    def _(step):
        atom_copy(step, from_slot(step)).start()

    def want_copy(step, slot_at):
        return remote(
            want_out.at[q_peer(step)], want_in.at[slot_at], want_send.at[step], want_recv.at[slot_at], at(my_z, q_peer(step))
        )

    @pl.loop(1, plane)
    def _(step):
        want_copy(step, my_q).start()

    want_in[my_q] = want_out[my_q]

    loads[4].wait()
    rev_cols[...] = hot(iota((edges, edges), 0) == reverse[...])

    @pl.loop(0, trip_count // chunk)
    def _(i):
        span = pl.ds(pl.multiple_of(i * chunk, chunk), chunk)
        rt[:, span] = dot(rev_cols[...], tt[:, span]).astype(BF16)

    loads[5].wait()
    loads[6].wait()
    bt[...] = dot(jnp.transpose(angle_w[...].astype(F32)).astype(BF16), angular[...])
    loads[7].wait()
    loads[8].wait()
    gate[...] = dot(jnp.transpose(radial[...].astype(F32)).astype(BF16), radial_w[...])

    @pl.loop(1, plane)
    def _(step):
        want_copy(step, q_peer(step)).wait_recv()

    for q in range(plane):
        picks = hot_rows(want_in[q], half * local)
        for part in range(2):
            sel[part, q * share : (q + 1) * share, :] = picks[part * share : (part + 1) * share]

    def rows_copy(part, step, slot_at):
        return remote(
            rows_out.at[part, q_peer(step)],
            rows_in.at[part, slot_at],
            rows_send.at[part, step],
            rows_recv.at[part, slot_at],
            at(my_z, q_peer(step)),
        )

    def send_rows(part):
        column_rows = table[part * half : (part + 1) * half].reshape(half * local, atom_width)
        rows = dot(sel[part], column_rows).astype(BF16)
        rows_out[part] = rows.reshape(plane, share, atom_width)

        @pl.loop(1, plane)
        def _(step):
            rows_copy(part, step, my_q).start()

        rows_in[part, my_q] = rows_out[part, my_q]

    def wait_atoms(slot_at):
        remote(atoms, table.at[slot_at], atom_send.at[0], atom_recv.at[slot_at], at(z_peer(1), my_q)).wait_recv()

    @pl.loop(1, half)
    def _(step):
        wait_atoms((own + step) % half)

    send_rows(0)

    for part in range(2):
        sel_t[part] = jnp.transpose(sel[part].astype(F32)).astype(BF16)
    loads[9].wait()
    down_t[...] = jnp.transpose(down_w[...].astype(F32)).astype(BF16)
    loads[11].wait()
    loads[12].wait()

    @pl.loop(0, width // tile)
    def _(i):
        span = pl.ds(pl.multiple_of(i * tile, tile), tile)
        pre[:, span] = dot(messages[...], message_w[:, span])

    @pl.loop(half, depth)
    def _(slot_at):
        wait_atoms(slot_at)

    send_rows(1)

    loads[10].wait()
    loads[14].wait()
    same = dot_nt(up_ca[...], up_ca[...]) + dot_nt(up_ac[...], up_ac[...])
    cross = dot_nt(up_ac[...], up_ca[...])
    cross = cross + jnp.transpose(cross)
    for part, value in enumerate((same, cross)):
        high = value.astype(BF16)
        mix[part, :tri, :] = high
        mix[part, tri:, :] = (value - high.astype(F32)).astype(BF16)
    loads[13].wait()
    loads[15].wait()

    end_rows = [None, None]
    for part in range(2):

        @pl.loop(1, plane)
        def _(step):
            rows_copy(part, step, q_peer(step)).wait_recv()

        slot_rows = rows_in[part].reshape(total, atom_width)
        for role in range(2):
            found = dot(edge_rows[role, :, part * total : (part + 1) * total], slot_rows)
            end_rows[role] = found if part == 0 else end_rows[role] + found
    source_rows, target_rows = end_rows[0].astype(BF16), end_rows[1].astype(BF16)
    down = jnp.zeros((tri, edges), F32)
    for start in range(0, width, tile):
        span = slice(start, start + tile)
        part = pre[:, span] + dot(source_rows, source_w[:, span]) + dot(target_rows, target_w[:, span])
        pre[:, span] = part
        hidden[:, span] = (part * jax.nn.sigmoid(part) * gate[:, span]).astype(BF16)
        down = down + dot_nt(down_t[:, span], hidden[:, span])
    reduced = (down * jax.nn.sigmoid(down)).astype(BF16)
    terms = (dot(reduced, st[...]) * bt[...]).astype(BF16)
    gathered = dot_nt(terms, tt[...]).astype(BF16)
    gather_out[...] = gathered

    pair_copy = remote(gather_out, gather_in, pair_send, pair_recv, at(my_z, my_q + 1 - 2 * (my_q % 2)))
    pair_copy.start()

    def mixed(part, value):
        both = dot(mix[part], value)
        return (both[:tri] + both[tri:]).astype(BF16)

    y[...] = dot(mixed(0, gathered), tt[...])
    sigma = jax.nn.sigmoid(down)
    down_slope = sigma * (1.0 + down * (1.0 - sigma))
    for start in range(0, width, tile):
        span = slice(start, start + tile)
        part = pre[:, span]
        sigma = jax.nn.sigmoid(part)
        gate[:, span] = gate[:, span] * (sigma * (1.0 + part * (1.0 - sigma)))

    pair_copy.wait_recv()

    terms = ((y[...] + dot(mixed(1, gather_in[...]), rt[...])) * bt[...]).astype(BF16)
    down_grad = dot_nt(terms, st[...]) * down_slope
    down_grad = jnp.transpose(down_grad).astype(BF16)
    ends = [jnp.zeros((edges, atom_width), F32) for _ in range(2)]
    for start in range(0, width, tile):
        span = slice(start, start + tile)
        part = (dot(down_grad, down_t[:, span]) * gate[:, span]).astype(BF16)
        grad[:, span] = part
        ends[0] = ends[0] + dot_nt(part, source_w[:, span])
        ends[1] = ends[1] + dot_nt(part, target_w[:, span])
    ends = jnp.concatenate([ends[0].astype(BF16), ends[1].astype(BF16)], axis=0)

    def back_copy(part, step, slot_at):
        return remote(
            back_out.at[part, q_peer(step)],
            back_in.at[part, slot_at],
            back_send.at[part, step],
            back_recv.at[part, slot_at],
            at(my_z, q_peer(step)),
        )

    for part in (1, 0):
        back = dot(slot_cols[part * total : (part + 1) * total, :], ends).astype(BF16)
        back_out[part] = back.reshape(plane, share, atom_width)

        @pl.loop(1, plane)
        def _(step):
            back_copy(part, step, my_q).start()

        back_in[part, my_q] = back_out[part, my_q]

    mine = jnp.transpose(gather_out[...].astype(F32)).astype(BF16)
    theirs = jnp.transpose(dot(gather_in[...], rev_cols[...])).astype(BF16)
    for start in range(0, width, tile):
        span = slice(start, start + tile)
        raised = dot(mine, up_ca[:, span]) + dot(theirs, up_ac[:, span])
        updated_out[:, span] = raised.astype(BF16)

    def part_copy(step, slot_at):
        return remote(
            part_out.at[to_slot(step)], part_in.at[slot_at], part_send.at[step], part_recv.at[slot_at], at(z_peer(step), my_q)
        )

    for part in (1, 0):

        @pl.loop(1, plane)
        def _(step):
            back_copy(part, step, q_peer(step)).wait_recv()

        sums = dot(sel_t[part], back_in[part].reshape(total, atom_width)).astype(BF16)
        part_out[part * half : (part + 1) * half] = sums.reshape(half, local, atom_width)

        @pl.loop(1 if part else half + 1, half + 1 if part else depth)
        def _(step):
            part_copy(step, from_slot(step)).start()

    part_in[own] = part_out[own]

    @pl.loop(0, width // tile)
    def _(i):
        span = pl.ds(pl.multiple_of(i * tile, tile), tile)
        message_out[:, span] = dot_nt(grad[...], message_w[span, :]).astype(BF16)

    @pl.loop(1, depth)
    def _(step):
        slot_at = (own + step) % depth
        remote(
            part_out.at[0], part_in.at[slot_at], part_send.at[0], part_recv.at[slot_at], at(z_peer(1), my_q)
        ).wait_recv()

    owned = part_in[0].astype(F32)
    for z in range(1, depth):
        owned = owned + part_in[z].astype(F32)
    atom_out[...] = owned

    @pl.loop(1, depth)
    def _(step):
        atom_copy(step, from_slot(step)).wait_send()
        part_copy(step, from_slot(step)).wait_send()

    @pl.loop(1, plane)
    def _(step):
        want_copy(step, my_q).wait_send()
        for part in range(2):
            rows_copy(part, step, my_q).wait_send()
            back_copy(part, step, my_q).wait_send()

    pair_copy.wait_send()


def shards(
    atoms,
    fetch_rows,
    edge_slots,
    messages,
    radial,
    angular,
    trip_edges,
    trip_blocks,
    reverse_slot,
    message_weight,
    source_weight,
    target_weight,
    radial_weight,
    down_weight,
    angle_weight,
    up_ca_weight,
    up_ac_weight,
):
    count = lax.axis_size("graph")
    plane = PLANE
    depth = count // plane
    local, atom_width = atoms.shape
    edges, width = messages.shape
    tri = down_weight.shape[1]
    trip_count = trip_edges.shape[1]
    per_peer = fetch_rows.shape[2]
    half = depth // 2
    share = half * per_peer
    total = plane * share
    fetch = jnp.transpose(fetch_rows[0])
    operands = (
        atoms,
        fetch,
        edge_slots,
        trip_edges,
        reverse_slot.reshape(1, edges),
        angular,
        angle_weight,
        radial,
        radial_weight,
        down_weight,
        up_ca_weight,
        messages,
        message_weight,
        source_weight,
        up_ac_weight,
        target_weight,
    )
    V = pltpu.VMEM
    DMA = pltpu.SemaphoreType.DMA
    scratch = [V(x.shape, x.dtype) for x in operands] + [
        V((edges, trip_count), BF16),
        V((edges, trip_count), BF16),
        V((tri, trip_count), F32),
        V((edges, width), F32),
        V((edges, width), F32),
        V((edges, width), BF16),
        V((edges, width), BF16),
        V((tri, width), BF16),
        V((edges, trip_count), BF16),
        V((tri, trip_count), F32),
        V((2, 2 * tri, tri), BF16),
        V((2, edges, 2 * total), BF16),
        V((2 * total, 2 * edges), BF16),
        V((edges, edges), BF16),
        V((2, total, half * local), BF16),
        V((2, half * local, total), BF16),
        V((tri, edges), BF16),
        V((depth, local, atom_width), BF16),
        V((plane, 1, 128), jnp.int32),
        V((plane, 1, 128), jnp.int32),
        V((2, plane, share, atom_width), BF16),
        V((2, plane, share, atom_width), BF16),
        V((tri, edges), BF16),
        V((2, plane, share, atom_width), BF16),
        V((2, plane, share, atom_width), BF16),
        V((depth, local, atom_width), BF16),
        V((depth, local, atom_width), BF16),
        V((1, 1), jnp.int32),
        DMA((17,)),
        DMA((depth,)),
        DMA((depth,)),
        DMA((plane,)),
        DMA((plane,)),
        DMA((2, plane)),
        DMA((2, plane)),
        DMA,
        DMA,
        DMA((2, plane)),
        DMA((2, plane)),
        DMA((depth,)),
        DMA((depth,)),
    ]
    return pl.pallas_call(
        functools.partial(kernel, plane, count),
        out_shape=(
            pltpu.VMEM((edges, width), BF16),
            pltpu.VMEM((edges, width), BF16),
            pltpu.VMEM((local, atom_width), F32),
        ),
        in_specs=[pl.BlockSpec(memory_space=pl.ANY)] * (1 + len(operands)),
        out_specs=[pl.BlockSpec(memory_space=pltpu.VMEM)] * 3,
        scratch_shapes=scratch,
        compiler_params=pltpu.CompilerParams(
            collective_id=0, has_side_effects=True, vmem_limit_bytes=VMEM
        ),
        cost_estimate=pl.CostEstimate(flops=3_000_000_000, bytes_accessed=8_000_000, transcendentals=1_000_000),
    )(trip_blocks.reshape(1, 1), *operands)


def solution(mesh):
    both = ("dp", "graph")
    rows, lanes = P(both, None), P(None, both)
    placed = (
        rows,
        P(both, None, None),
        lanes,
        rows,
        lanes,
        lanes,
        lanes,
        P(both),
        P(both),
    ) + (P(),) * 8
    return jax.shard_map(
        shards,
        mesh=mesh,
        in_specs=placed,
        out_specs=(rows, rows, rows),
        check_vma=False,
    )
```

```python
import functools

import jax
import jax.numpy as jnp
from jax import lax
from jax.experimental import pallas as pl
from jax.experimental.pallas import tpu as pltpu
from jax.sharding import PartitionSpec as P

TBLK = 256
PLANE = 8
VMEM = 56 * 1024 * 1024
F32 = jnp.float32
BF16 = jnp.bfloat16
MESH = pl.DeviceIdType.MESH


def iota(shape, dim):
    return lax.broadcasted_iota(jnp.int32, shape, dim)


def dot(left, right):
    return jnp.dot(left, right, preferred_element_type=F32)


def dot_nt(left, right):
    return lax.dot_general(left, right, (((1,), (1,)), ((), ())), preferred_element_type=F32)


def hot(mask):
    return jnp.where(mask, 1.0, 0.0).astype(BF16)


def column(row):
    count = row.shape[1]
    tall = jnp.broadcast_to(row.astype(F32), (128, count))
    return jnp.transpose(tall)


def hot_rows(row, width):
    wide = column(row).astype(jnp.int32)
    parts = [hot(wide == iota(wide.shape, 1) + start) for start in range(0, width, 128)]
    return jnp.concatenate(parts, axis=1)


def kernel(
    plane,
    count,
    *refs,
):
    n_in = 16
    blocks_hbm, *hbm = refs[: n_in + 1]
    updated_out, message_out, atom_out = refs[n_in + 1 : n_in + 4]
    vm = refs[n_in + 4 : 2 * n_in + 4]
    (
        atoms,
        fetch,
        slots_in,
        trips,
        reverse,
        angular,
        angle_w,
        radial,
        radial_w,
        down_w,
        up_ca,
        messages,
        message_w,
        source_w,
        up_ac,
        target_w,
    ) = vm
    (
        st,
        tt,
        bt,
        gate,
        pre,
        hidden,
        grad,
        down_t,
        rt,
        y,
        mix,
        edge_rows,
        slot_cols,
        rev_cols,
        sel,
        sel_t,
        gather_out,
        table,
        want_out,
        want_in,
        rows_out,
        rows_in,
        gather_in,
        back_out,
        back_in,
        part_out,
        part_in,
        blocks,
        in_sem,
        atom_send,
        atom_recv,
        want_send,
        want_recv,
        rows_send,
        rows_recv,
        pair_send,
        pair_recv,
        back_send,
        back_recv,
        part_send,
        part_recv,
    ) = refs[2 * n_in + 4 :]
    depth = count // plane
    half = depth // 2
    own = half // 2
    per_peer = fetch.shape[0]
    local, atom_width = atoms.shape
    share = half * per_peer
    total = plane * share
    edges, width = messages.shape
    trip_count = trips.shape[1]
    tri = down_w.shape[1]
    tile = 256

    me = lax.axis_index("graph")
    my_z, my_q = me // plane, me % plane

    def far_first(step, size):
        return size // 2 + (step // 2) * (2 * (step % 2) - 1)

    def z_peer(step):
        return (my_z + far_first(step, depth)) % depth

    def q_peer(step):
        return (my_q + far_first(step, plane)) % plane

    def to_slot(step):
        return (own + far_first(step, depth)) % depth

    def from_slot(step):
        return (own - far_first(step, depth) + depth) % depth

    def at(z, q):
        return {"graph": z * plane + q}

    def remote(src, dst, send, recv, where):
        return pltpu.make_async_remote_copy(
            src_ref=src, dst_ref=dst, send_sem=send, recv_sem=recv, device_id=where, device_id_type=MESH
        )

    def wait_recv(group, recv):
        remote(group, group, atom_send, recv, at(z_peer(1), my_q)).wait_recv()

    def wait_send(group, send):
        remote(group, group, send, atom_recv.at[0], at(z_peer(1), my_q)).wait_send()

    barrier = pltpu.get_barrier_semaphore()

    @pl.loop(1, depth)
    def _(step):
        pl.semaphore_signal(barrier, inc=1, device_id=at(z_peer(step), my_q), device_id_type=MESH)

    @pl.loop(1, plane)
    def _(step):
        pl.semaphore_signal(barrier, inc=1, device_id=at(my_z, q_peer(step)), device_id_type=MESH)

    loads = [pltpu.make_async_copy(hbm[i], vm[i], in_sem.at[i]) for i in range(n_in)]
    loads.append(pltpu.make_async_copy(blocks_hbm, blocks, in_sem.at[n_in]))
    for load in [loads[n_in]] + loads[:n_in]:
        load.start()

    loads[1].wait()
    flat = jnp.concatenate([fetch[c : c + 1, :] for c in range(per_peer)], axis=1)
    flat = jnp.broadcast_to(flat.astype(F32), (8, per_peer * count)).astype(BF16)
    from_peer = iota((per_peer * count, 128), 0)
    to_lane = iota((per_peer * count, 128), 1)
    lane_z = (my_z + (to_lane // share) * half + to_lane % half + depth - own) % depth
    lane_c = (to_lane % share) // half
    same_c = from_peer // count == lane_c
    offset = from_peer % count - lane_z * plane
    lane = iota((8, 128), 1)
    for q in range(plane):
        pick = hot(same_c & (offset == q))
        ids = dot(flat, pick).astype(jnp.int32) + (lane % half) * local
        want_out[q] = jnp.where(lane < 2 * share, ids, -1)[0:1, :]

    loads[2].wait()
    slot = slots_in[...]
    owner = slot // per_peer
    place = (owner // plane - my_z + own + depth) % depth
    slot = (place // half) * total + (owner % plane) * share + (slot % per_peer) * half + place % half
    for role in range(2):
        row = slot[role : role + 1, :]
        edge_rows[role] = hot_rows(row, 2 * total)
        slot_cols[:, role * edges : (role + 1) * edges] = hot(iota((2 * total, edges), 0) == row)

    loads[n_in].wait()
    loads[3].wait()
    live = blocks[...] * TBLK
    chunk = 512

    @pl.loop(0, trip_count // chunk)
    def _(i):
        span = pl.ds(pl.multiple_of(i * chunk, chunk), chunk)
        edge = iota((edges, chunk), 0)
        at_trip = iota((1, chunk), 1) + i * chunk
        targets = jnp.where(at_trip < live, trips[0:1, span], -1)
        tt[:, span] = hot(edge == targets)
        st[:, span] = hot(edge == trips[1:2, span])

    loads[0].wait()
    table[own] = atoms[...]

    pl.semaphore_wait(barrier, depth + plane - 2)

    def atom_copy(step, slot_at):
        return remote(atoms, table.at[slot_at], atom_send, atom_recv.at[slot_at // half], at(z_peer(step), my_q))

    @pl.loop(1, depth)
    def _(step):
        atom_copy(step, from_slot(step)).start()

    def want_copy(step, slot_at):
        return remote(
            want_out.at[q_peer(step)], want_in.at[slot_at], want_send, want_recv, at(my_z, q_peer(step))
        )

    @pl.loop(1, plane)
    def _(step):
        want_copy(step, my_q).start()

    want_in[my_q] = want_out[my_q]

    loads[4].wait()
    rev_cols[...] = hot(iota((edges, edges), 0) == reverse[...])

    @pl.loop(0, trip_count // chunk)
    def _(i):
        span = pl.ds(pl.multiple_of(i * chunk, chunk), chunk)
        rt[:, span] = dot(rev_cols[...], tt[:, span]).astype(BF16)

    loads[5].wait()
    loads[6].wait()
    bt[...] = dot(jnp.transpose(angle_w[...].astype(F32)).astype(BF16), angular[...])
    loads[7].wait()
    loads[8].wait()
    gate[...] = dot(jnp.transpose(radial[...].astype(F32)).astype(BF16), radial_w[...])

    wait_recv(want_in.at[pl.ds(0, plane - 1)], want_recv)

    for q in range(plane):
        picks = hot_rows(want_in[q], half * local)
        for part in range(2):
            sel[part, q * share : (q + 1) * share, :] = picks[part * share : (part + 1) * share]

    def rows_copy(part, step, slot_at):
        return remote(
            rows_out.at[part, q_peer(step)],
            rows_in.at[part, slot_at],
            rows_send.at[part],
            rows_recv.at[part],
            at(my_z, q_peer(step)),
        )

    def send_rows(part):
        column_rows = table[part * half : (part + 1) * half].reshape(half * local, atom_width)
        rows = dot(sel[part], column_rows).astype(BF16)
        rows_out[part] = rows.reshape(plane, share, atom_width)

        @pl.loop(1, plane)
        def _(step):
            rows_copy(part, step, my_q).start()

        rows_in[part, my_q] = rows_out[part, my_q]

    wait_recv(table.at[pl.ds(0, half - 1)], atom_recv.at[0])
    send_rows(0)

    for part in range(2):
        sel_t[part] = jnp.transpose(sel[part].astype(F32)).astype(BF16)
    loads[9].wait()
    down_t[...] = jnp.transpose(down_w[...].astype(F32)).astype(BF16)
    loads[11].wait()
    loads[12].wait()

    @pl.loop(0, width // tile)
    def _(i):
        span = pl.ds(pl.multiple_of(i * tile, tile), tile)
        pre[:, span] = dot(messages[...], message_w[:, span])

    wait_recv(table.at[pl.ds(half, half)], atom_recv.at[1])

    send_rows(1)

    loads[10].wait()
    loads[14].wait()
    same = dot_nt(up_ca[...], up_ca[...]) + dot_nt(up_ac[...], up_ac[...])
    cross = dot_nt(up_ac[...], up_ca[...])
    cross = cross + jnp.transpose(cross)
    for part, value in enumerate((same, cross)):
        high = value.astype(BF16)
        mix[part, :tri, :] = high
        mix[part, tri:, :] = (value - high.astype(F32)).astype(BF16)
    loads[13].wait()
    loads[15].wait()

    end_rows = [None, None]
    for part in range(2):
        wait_recv(rows_in.at[part, pl.ds(0, plane - 1)], rows_recv.at[part])
        slot_rows = rows_in[part].reshape(total, atom_width)
        for role in range(2):
            found = dot(edge_rows[role, :, part * total : (part + 1) * total], slot_rows)
            end_rows[role] = found if part == 0 else end_rows[role] + found
    source_rows, target_rows = end_rows[0].astype(BF16), end_rows[1].astype(BF16)
    down = jnp.zeros((tri, edges), F32)
    for start in range(0, width, tile):
        span = slice(start, start + tile)
        part = pre[:, span] + dot(source_rows, source_w[:, span]) + dot(target_rows, target_w[:, span])
        pre[:, span] = part
        hidden[:, span] = (part * jax.nn.sigmoid(part) * gate[:, span]).astype(BF16)
        down = down + dot_nt(down_t[:, span], hidden[:, span])
    reduced = (down * jax.nn.sigmoid(down)).astype(BF16)
    terms = (dot(reduced, st[...]) * bt[...]).astype(BF16)
    gathered = dot_nt(terms, tt[...]).astype(BF16)
    gather_out[...] = gathered

    pair_copy = remote(gather_out, gather_in, pair_send, pair_recv, at(my_z, my_q + 1 - 2 * (my_q % 2)))
    pair_copy.start()

    def mixed(part, value):
        both = dot(mix[part], value)
        return (both[:tri] + both[tri:]).astype(BF16)

    y[...] = dot(mixed(0, gathered), tt[...])
    sigma = jax.nn.sigmoid(down)
    down_slope = sigma * (1.0 + down * (1.0 - sigma))
    for start in range(0, width, tile):
        span = slice(start, start + tile)
        part = pre[:, span]
        sigma = jax.nn.sigmoid(part)
        gate[:, span] = gate[:, span] * (sigma * (1.0 + part * (1.0 - sigma)))

    pair_copy.wait_recv()

    terms = ((y[...] + dot(mixed(1, gather_in[...]), rt[...])) * bt[...]).astype(BF16)
    down_grad = dot_nt(terms, st[...]) * down_slope
    down_grad = jnp.transpose(down_grad).astype(BF16)
    ends = [jnp.zeros((edges, atom_width), F32) for _ in range(2)]
    for start in range(0, width, tile):
        span = slice(start, start + tile)
        part = (dot(down_grad, down_t[:, span]) * gate[:, span]).astype(BF16)
        grad[:, span] = part
        ends[0] = ends[0] + dot_nt(part, source_w[:, span])
        ends[1] = ends[1] + dot_nt(part, target_w[:, span])
    ends = jnp.concatenate([ends[0].astype(BF16), ends[1].astype(BF16)], axis=0)

    def back_copy(part, step, slot_at):
        return remote(
            back_out.at[part, q_peer(step)],
            back_in.at[part, slot_at],
            back_send.at[part],
            back_recv.at[part],
            at(my_z, q_peer(step)),
        )

    for part in (1, 0):
        back = dot(slot_cols[part * total : (part + 1) * total, :], ends).astype(BF16)
        back_out[part] = back.reshape(plane, share, atom_width)

        @pl.loop(1, plane)
        def _(step):
            back_copy(part, step, my_q).start()

        back_in[part, my_q] = back_out[part, my_q]

    mine = jnp.transpose(gather_out[...].astype(F32)).astype(BF16)
    theirs = jnp.transpose(dot(gather_in[...], rev_cols[...])).astype(BF16)
    for start in range(0, width, tile):
        span = slice(start, start + tile)
        raised = dot(mine, up_ca[:, span]) + dot(theirs, up_ac[:, span])
        updated_out[:, span] = raised.astype(BF16)

    def part_copy(step, slot_at):
        return remote(
            part_out.at[to_slot(step)], part_in.at[slot_at], part_send, part_recv, at(z_peer(step), my_q)
        )

    for part in (1, 0):
        wait_recv(back_in.at[part, pl.ds(0, plane - 1)], back_recv.at[part])
        sums = dot(sel_t[part], back_in[part].reshape(total, atom_width)).astype(BF16)
        part_out[part * half : (part + 1) * half] = sums.reshape(half, local, atom_width)

        @pl.loop(1 if part else half + 1, half + 1 if part else depth)
        def _(step):
            part_copy(step, from_slot(step)).start()

    part_in[own] = part_out[own]

    @pl.loop(0, width // tile)
    def _(i):
        span = pl.ds(pl.multiple_of(i * tile, tile), tile)
        message_out[:, span] = dot_nt(grad[...], message_w[span, :]).astype(BF16)

    wait_recv(part_in.at[pl.ds(0, depth - 1)], part_recv)

    owned = part_in[0].astype(F32)
    for z in range(1, depth):
        owned = owned + part_in[z].astype(F32)
    atom_out[...] = owned

    wait_send(table.at[pl.ds(0, depth - 1)], atom_send)
    wait_send(want_out.at[pl.ds(0, plane - 1)], want_send)
    for part in range(2):
        wait_send(rows_out.at[part, pl.ds(0, plane - 1)], rows_send.at[part])
        wait_send(back_out.at[part, pl.ds(0, plane - 1)], back_send.at[part])
    wait_send(part_out.at[pl.ds(0, depth - 1)], part_send)
    pair_copy.wait_send()


def shards(
    atoms,
    fetch_rows,
    edge_slots,
    messages,
    radial,
    angular,
    trip_edges,
    trip_blocks,
    reverse_slot,
    message_weight,
    source_weight,
    target_weight,
    radial_weight,
    down_weight,
    angle_weight,
    up_ca_weight,
    up_ac_weight,
):
    count = lax.axis_size("graph")
    plane = PLANE
    depth = count // plane
    local, atom_width = atoms.shape
    edges, width = messages.shape
    tri = down_weight.shape[1]
    trip_count = trip_edges.shape[1]
    per_peer = fetch_rows.shape[2]
    half = depth // 2
    share = half * per_peer
    total = plane * share
    fetch = jnp.transpose(fetch_rows[0])
    operands = (
        atoms,
        fetch,
        edge_slots,
        trip_edges,
        reverse_slot.reshape(1, edges),
        angular,
        angle_weight,
        radial,
        radial_weight,
        down_weight,
        up_ca_weight,
        messages,
        message_weight,
        source_weight,
        up_ac_weight,
        target_weight,
    )
    V = pltpu.VMEM
    DMA = pltpu.SemaphoreType.DMA
    scratch = [V(x.shape, x.dtype) for x in operands] + [
        V((edges, trip_count), BF16),
        V((edges, trip_count), BF16),
        V((tri, trip_count), F32),
        V((edges, width), F32),
        V((edges, width), F32),
        V((edges, width), BF16),
        V((edges, width), BF16),
        V((tri, width), BF16),
        V((edges, trip_count), BF16),
        V((tri, trip_count), F32),
        V((2, 2 * tri, tri), BF16),
        V((2, edges, 2 * total), BF16),
        V((2 * total, 2 * edges), BF16),
        V((edges, edges), BF16),
        V((2, total, half * local), BF16),
        V((2, half * local, total), BF16),
        V((tri, edges), BF16),
        V((depth, local, atom_width), BF16),
        V((plane, 1, 128), jnp.int32),
        V((plane, 1, 128), jnp.int32),
        V((2, plane, share, atom_width), BF16),
        V((2, plane, share, atom_width), BF16),
        V((tri, edges), BF16),
        V((2, plane, share, atom_width), BF16),
        V((2, plane, share, atom_width), BF16),
        V((depth, local, atom_width), BF16),
        V((depth, local, atom_width), BF16),
        V((1, 1), jnp.int32),
        DMA((17,)),
        DMA,
        DMA((2,)),
        DMA,
        DMA,
        DMA((2,)),
        DMA((2,)),
        DMA,
        DMA,
        DMA((2,)),
        DMA((2,)),
        DMA,
        DMA,
    ]
    return pl.pallas_call(
        functools.partial(kernel, plane, count),
        out_shape=(
            pltpu.VMEM((edges, width), BF16),
            pltpu.VMEM((edges, width), BF16),
            pltpu.VMEM((local, atom_width), F32),
        ),
        in_specs=[pl.BlockSpec(memory_space=pl.ANY)] * (1 + len(operands)),
        out_specs=[pl.BlockSpec(memory_space=pltpu.VMEM)] * 3,
        scratch_shapes=scratch,
        compiler_params=pltpu.CompilerParams(
            collective_id=0, has_side_effects=True, vmem_limit_bytes=VMEM
        ),
        cost_estimate=pl.CostEstimate(flops=3_000_000_000, bytes_accessed=8_000_000, transcendentals=1_000_000),
    )(trip_blocks.reshape(1, 1), *operands)


def solution(mesh):
    both = ("dp", "graph")
    rows, lanes = P(both, None), P(None, both)
    placed = (
        rows,
        P(both, None, None),
        lanes,
        rows,
        lanes,
        lanes,
        lanes,
        P(both),
        P(both),
    ) + (P(),) * 8
    return jax.shard_map(
        shards,
        mesh=mesh,
        in_specs=placed,
        out_specs=(rows, rows, rows),
        check_vma=False,
    )
```

```python
import functools

import jax
import jax.numpy as jnp
from jax import lax
from jax.experimental import pallas as pl
from jax.experimental.pallas import tpu as pltpu
from jax.sharding import PartitionSpec as P

TBLK = 256
PLANE = 8
VMEM = 56 * 1024 * 1024
F32 = jnp.float32
BF16 = jnp.bfloat16
MESH = pl.DeviceIdType.MESH


def iota(shape, dim):
    return lax.broadcasted_iota(jnp.int32, shape, dim)


def dot(left, right):
    return jnp.dot(left, right, preferred_element_type=F32)


def dot_nt(left, right):
    return lax.dot_general(left, right, (((1,), (1,)), ((), ())), preferred_element_type=F32)


def hot(mask):
    return jnp.where(mask, 1.0, 0.0).astype(BF16)


def column(row):
    count = row.shape[1]
    tall = jnp.broadcast_to(row.astype(F32), (128, count))
    return jnp.transpose(tall)


def hot_rows(row, width):
    wide = column(row).astype(jnp.int32)
    parts = [hot(wide == iota(wide.shape, 1) + start) for start in range(0, width, 128)]
    return jnp.concatenate(parts, axis=1)


def kernel(
    plane,
    count,
    *refs,
):
    n_in = 16
    blocks_hbm, *hbm = refs[: n_in + 1]
    edge_out, atom_out = refs[n_in + 1 : n_in + 3]
    vm = refs[n_in + 3 : 2 * n_in + 3]
    (
        atoms,
        fetch,
        slots_in,
        trips,
        reverse,
        angular,
        angle_w,
        radial,
        radial_w,
        down_w,
        up_ca,
        messages,
        message_w,
        source_w,
        up_ac,
        target_w,
    ) = vm
    (
        st,
        tt,
        bt,
        gate,
        pre,
        hidden,
        grad,
        down_t,
        tn,
        sn,
        rt,
        y,
        mix,
        edge_rows,
        slot_cols,
        rev_cols,
        sel,
        sel_t,
        gather_out,
        table,
        want_out,
        want_in,
        rows_out,
        rows_in,
        gather_in,
        back_out,
        back_in,
        part_out,
        part_in,
        blocks,
        in_sem,
        atom_send,
        atom_recv,
        want_send,
        want_recv,
        rows_send,
        rows_recv,
        pair_send,
        pair_recv,
        back_send,
        back_recv,
        part_send,
        part_recv,
    ) = refs[2 * n_in + 3 :]
    depth = count // plane
    half = depth // 2
    own = half // 2
    per_peer = fetch.shape[0]
    local, atom_width = atoms.shape
    share = half * per_peer
    total = plane * share
    edges, width = messages.shape
    trip_count = trips.shape[1]
    tri = down_w.shape[1]
    tile = 256

    me = lax.axis_index("graph")
    my_z, my_q = me // plane, me % plane

    def far_first(step, size):
        return size // 2 + (step // 2) * (2 * (step % 2) - 1)

    def z_peer(step):
        return (my_z + far_first(step, depth)) % depth

    def q_peer(step):
        return (my_q + far_first(step, plane)) % plane

    def to_slot(step):
        return (own + far_first(step, depth)) % depth

    def from_slot(step):
        return (own - far_first(step, depth) + depth) % depth

    def at(z, q):
        return {"graph": z * plane + q}

    def remote(src, dst, send, recv, where):
        return pltpu.make_async_remote_copy(
            src_ref=src, dst_ref=dst, send_sem=send, recv_sem=recv, device_id=where, device_id_type=MESH
        )

    def wait_recv(group, recv):
        remote(group, group, atom_send, recv, at(z_peer(1), my_q)).wait_recv()

    def wait_send(group, send):
        remote(group, group, send, atom_recv.at[0], at(z_peer(1), my_q)).wait_send()

    barrier = pltpu.get_barrier_semaphore()

    @pl.loop(1, depth)
    def _(step):
        pl.semaphore_signal(barrier, inc=1, device_id=at(z_peer(step), my_q), device_id_type=MESH)

    @pl.loop(1, plane)
    def _(step):
        pl.semaphore_signal(barrier, inc=1, device_id=at(my_z, q_peer(step)), device_id_type=MESH)

    loads = [pltpu.make_async_copy(hbm[i], vm[i], in_sem.at[i]) for i in range(n_in)]
    loads.append(pltpu.make_async_copy(blocks_hbm, blocks, in_sem.at[n_in]))
    for load in [loads[n_in]] + loads[:n_in]:
        load.start()

    loads[1].wait()
    flat = jnp.concatenate([fetch[c : c + 1, :] for c in range(per_peer)], axis=1)
    flat = jnp.broadcast_to(flat.astype(F32), (8, per_peer * count)).astype(BF16)
    from_peer = iota((per_peer * count, 128), 0)
    to_lane = iota((per_peer * count, 128), 1)
    lane_z = (my_z + (to_lane // share) * half + to_lane % half + depth - own) % depth
    lane_c = (to_lane % share) // half
    same_c = from_peer // count == lane_c
    offset = from_peer % count - lane_z * plane
    lane = iota((8, 128), 1)
    for q in range(plane):
        pick = hot(same_c & (offset == q))
        ids = dot(flat, pick).astype(jnp.int32) + (lane % half) * local
        want_out[q] = jnp.where(lane < 2 * share, ids, -1)[0:1, :]

    loads[2].wait()
    slot = slots_in[...]
    owner = slot // per_peer
    place = (owner // plane - my_z + own + depth) % depth
    slot = (place // half) * total + (owner % plane) * share + (slot % per_peer) * half + place % half
    for role in range(2):
        row = slot[role : role + 1, :]
        edge_rows[role] = hot_rows(row, 2 * total)
        slot_cols[:, role * edges : (role + 1) * edges] = hot(iota((2 * total, edges), 0) == row)

    loads[n_in].wait()
    loads[3].wait()
    live = blocks[...] * TBLK
    chunk = 512

    @pl.loop(0, trip_count // chunk)
    def _(i):
        span = pl.ds(pl.multiple_of(i * chunk, chunk), chunk)
        edge = iota((edges, chunk), 0)
        at_trip = iota((1, chunk), 1) + i * chunk
        targets = jnp.where(at_trip < live, trips[0:1, span], -1)
        tt[:, span] = hot(edge == targets)
        st[:, span] = hot(edge == trips[1:2, span])

    loads[0].wait()
    table[own] = atoms[...]

    pl.semaphore_wait(barrier, depth + plane - 2)

    def atom_copy(step, slot_at):
        return remote(atoms, table.at[slot_at], atom_send, atom_recv.at[slot_at // half], at(z_peer(step), my_q))

    @pl.loop(1, depth)
    def _(step):
        atom_copy(step, from_slot(step)).start()

    def want_copy(step, slot_at):
        return remote(
            want_out.at[q_peer(step)], want_in.at[slot_at], want_send, want_recv, at(my_z, q_peer(step))
        )

    @pl.loop(1, plane)
    def _(step):
        want_copy(step, my_q).start()

    want_in[my_q] = want_out[my_q]

    @pl.loop(0, trip_count // chunk)
    def _(i):
        span = pl.ds(pl.multiple_of(i * chunk, chunk), chunk)
        at_trip = iota((1, chunk), 1) + i * chunk
        tn[span, :] = hot_rows(jnp.where(at_trip < live, trips[0:1, span], -1), edges)
        sn[span, :] = hot_rows(trips[1:2, span], edges)

    loads[4].wait()
    rev_cols[...] = hot(iota((edges, edges), 0) == reverse[...])

    @pl.loop(0, trip_count // chunk)
    def _(i):
        span = pl.ds(pl.multiple_of(i * chunk, chunk), chunk)
        rt[:, span] = dot(rev_cols[...], tt[:, span]).astype(BF16)

    loads[5].wait()
    loads[6].wait()
    bt[...] = dot(jnp.transpose(angle_w[...].astype(F32)).astype(BF16), angular[...])
    loads[7].wait()
    loads[8].wait()
    gate[...] = dot(jnp.transpose(radial[...].astype(F32)).astype(BF16), radial_w[...])

    wait_recv(want_in.at[pl.ds(0, plane - 1)], want_recv)

    for q in range(plane):
        picks = hot_rows(want_in[q], half * local)
        for part in range(2):
            sel[part, q * share : (q + 1) * share, :] = picks[part * share : (part + 1) * share]

    def rows_copy(part, step, slot_at):
        return remote(
            rows_out.at[part, q_peer(step)],
            rows_in.at[part, slot_at],
            rows_send.at[part],
            rows_recv.at[part],
            at(my_z, q_peer(step)),
        )

    def send_rows(part):
        column_rows = table[part * half : (part + 1) * half].reshape(half * local, atom_width)
        rows = dot(sel[part], column_rows).astype(BF16)
        rows_out[part] = rows.reshape(plane, share, atom_width)

        @pl.loop(1, plane)
        def _(step):
            rows_copy(part, step, my_q).start()

        rows_in[part, my_q] = rows_out[part, my_q]

    wait_recv(table.at[pl.ds(0, half - 1)], atom_recv.at[0])
    send_rows(0)

    for part in range(2):
        sel_t[part] = jnp.transpose(sel[part].astype(F32)).astype(BF16)
    loads[9].wait()
    down_t[...] = jnp.transpose(down_w[...].astype(F32)).astype(BF16)
    loads[11].wait()
    loads[12].wait()

    @pl.loop(0, width // tile)
    def _(i):
        span = pl.ds(pl.multiple_of(i * tile, tile), tile)
        pre[:, span] = dot(messages[...], message_w[:, span])

    wait_recv(table.at[pl.ds(half, half)], atom_recv.at[1])

    send_rows(1)

    loads[10].wait()
    loads[14].wait()
    same = dot_nt(up_ca[...], up_ca[...]) + dot_nt(up_ac[...], up_ac[...])
    cross = dot_nt(up_ac[...], up_ca[...])
    cross = cross + jnp.transpose(cross)
    for part, value in enumerate((same, cross)):
        high = value.astype(BF16)
        mix[part, :tri, :] = high
        mix[part, tri:, :] = (value - high.astype(F32)).astype(BF16)
    loads[13].wait()
    loads[15].wait()

    end_rows = [None, None]
    for part in range(2):
        wait_recv(rows_in.at[part, pl.ds(0, plane - 1)], rows_recv.at[part])
        slot_rows = rows_in[part].reshape(total, atom_width)
        for role in range(2):
            found = dot(edge_rows[role, :, part * total : (part + 1) * total], slot_rows)
            end_rows[role] = found if part == 0 else end_rows[role] + found
    source_rows, target_rows = end_rows[0].astype(BF16), end_rows[1].astype(BF16)
    down = jnp.zeros((tri, edges), F32)
    for start in range(0, width, tile):
        span = slice(start, start + tile)
        part = pre[:, span] + dot(source_rows, source_w[:, span]) + dot(target_rows, target_w[:, span])
        pre[:, span] = part
        hidden[:, span] = (part * jax.nn.sigmoid(part) * gate[:, span]).astype(BF16)
        down = down + dot_nt(down_t[:, span], hidden[:, span])
    reduced = (down * jax.nn.sigmoid(down)).astype(BF16)
    terms = (dot(reduced, st[...]) * bt[...]).astype(BF16)
    gathered = dot(terms, tn[...]).astype(BF16)
    gather_out[...] = gathered

    pair_copy = remote(gather_out, gather_in, pair_send, pair_recv, at(my_z, my_q + 1 - 2 * (my_q % 2)))
    pair_copy.start()

    def mixed(part, value):
        both = dot(mix[part], value)
        return (both[:tri] + both[tri:]).astype(BF16)

    y[...] = dot(mixed(0, gathered), tt[...])
    sigma = jax.nn.sigmoid(down)
    down_slope = sigma * (1.0 + down * (1.0 - sigma))
    for start in range(0, width, tile):
        span = slice(start, start + tile)
        part = pre[:, span]
        sigma = jax.nn.sigmoid(part)
        gate[:, span] = gate[:, span] * (sigma * (1.0 + part * (1.0 - sigma)))

    pair_copy.wait_recv()

    terms = ((y[...] + dot(mixed(1, gather_in[...]), rt[...])) * bt[...]).astype(BF16)
    down_grad = dot(terms, sn[...]) * down_slope
    down_grad = jnp.transpose(down_grad).astype(BF16)
    ends = [jnp.zeros((edges, atom_width), F32) for _ in range(2)]
    for start in range(0, width, tile):
        span = slice(start, start + tile)
        part = (dot(down_grad, down_t[:, span]) * gate[:, span]).astype(BF16)
        grad[:, span] = part
        ends[0] = ends[0] + dot_nt(part, source_w[:, span])
        ends[1] = ends[1] + dot_nt(part, target_w[:, span])
    ends = jnp.concatenate([ends[0].astype(BF16), ends[1].astype(BF16)], axis=0)

    def back_copy(part, step, slot_at):
        return remote(
            back_out.at[part, q_peer(step)],
            back_in.at[part, slot_at],
            back_send.at[part],
            back_recv.at[part],
            at(my_z, q_peer(step)),
        )

    for part in (1, 0):
        back = dot(slot_cols[part * total : (part + 1) * total, :], ends).astype(BF16)
        back_out[part] = back.reshape(plane, share, atom_width)

        @pl.loop(1, plane)
        def _(step):
            back_copy(part, step, my_q).start()

        back_in[part, my_q] = back_out[part, my_q]

    mine = jnp.transpose(gather_out[...].astype(F32)).astype(BF16)
    theirs = jnp.transpose(dot(gather_in[...], rev_cols[...])).astype(BF16)
    for start in range(0, width, tile):
        span = slice(start, start + tile)
        raised = dot(mine, up_ca[:, span]) + dot(theirs, up_ac[:, span])
        edge_out[:edges, span] = raised.astype(BF16)

    def part_copy(step, slot_at):
        return remote(
            part_out.at[to_slot(step)], part_in.at[slot_at], part_send, part_recv, at(z_peer(step), my_q)
        )

    for part in (1, 0):
        wait_recv(back_in.at[part, pl.ds(0, plane - 1)], back_recv.at[part])
        sums = dot(sel_t[part], back_in[part].reshape(total, atom_width)).astype(BF16)
        part_out[part * half : (part + 1) * half] = sums.reshape(half, local, atom_width)

        @pl.loop(1 if part else half + 1, half + 1 if part else depth)
        def _(step):
            part_copy(step, from_slot(step)).start()

    part_in[own] = part_out[own]

    @pl.loop(0, width // tile)
    def _(i):
        span = pl.ds(pl.multiple_of(i * tile, tile), tile)
        edge_out[edges:, span] = dot_nt(grad[...], message_w[span, :]).astype(BF16)

    wait_recv(part_in.at[pl.ds(0, depth - 1)], part_recv)

    owned = part_in[0].astype(F32)
    for z in range(1, depth):
        owned = owned + part_in[z].astype(F32)
    atom_out[...] = owned

    wait_send(table.at[pl.ds(0, depth - 1)], atom_send)
    wait_send(want_out.at[pl.ds(0, plane - 1)], want_send)
    for part in range(2):
        wait_send(rows_out.at[part, pl.ds(0, plane - 1)], rows_send.at[part])
        wait_send(back_out.at[part, pl.ds(0, plane - 1)], back_send.at[part])
    wait_send(part_out.at[pl.ds(0, depth - 1)], part_send)
    pair_copy.wait_send()


def shards(
    atoms,
    fetch_rows,
    edge_slots,
    messages,
    radial,
    angular,
    trip_edges,
    trip_blocks,
    reverse_slot,
    message_weight,
    source_weight,
    target_weight,
    radial_weight,
    down_weight,
    angle_weight,
    up_ca_weight,
    up_ac_weight,
):
    count = lax.axis_size("graph")
    plane = PLANE
    depth = count // plane
    local, atom_width = atoms.shape
    edges, width = messages.shape
    tri = down_weight.shape[1]
    trip_count = trip_edges.shape[1]
    per_peer = fetch_rows.shape[2]
    half = depth // 2
    share = half * per_peer
    total = plane * share
    fetch = jnp.transpose(fetch_rows[0])
    operands = (
        atoms,
        fetch,
        edge_slots,
        trip_edges,
        reverse_slot.reshape(1, edges),
        angular,
        angle_weight,
        radial,
        radial_weight,
        down_weight,
        up_ca_weight,
        messages,
        message_weight,
        source_weight,
        up_ac_weight,
        target_weight,
    )
    V = pltpu.VMEM
    DMA = pltpu.SemaphoreType.DMA
    scratch = [V(x.shape, x.dtype) for x in operands] + [
        V((edges, trip_count), BF16),
        V((edges, trip_count), BF16),
        V((tri, trip_count), F32),
        V((edges, width), F32),
        V((edges, width), F32),
        V((edges, width), BF16),
        V((edges, width), BF16),
        V((tri, width), BF16),
        V((trip_count, edges), BF16),
        V((trip_count, edges), BF16),
        V((edges, trip_count), BF16),
        V((tri, trip_count), F32),
        V((2, 2 * tri, tri), BF16),
        V((2, edges, 2 * total), BF16),
        V((2 * total, 2 * edges), BF16),
        V((edges, edges), BF16),
        V((2, total, half * local), BF16),
        V((2, half * local, total), BF16),
        V((tri, edges), BF16),
        V((depth, local, atom_width), BF16),
        V((plane, 1, 128), jnp.int32),
        V((plane, 1, 128), jnp.int32),
        V((2, plane, share, atom_width), BF16),
        V((2, plane, share, atom_width), BF16),
        V((tri, edges), BF16),
        V((2, plane, share, atom_width), BF16),
        V((2, plane, share, atom_width), BF16),
        V((depth, local, atom_width), BF16),
        V((depth, local, atom_width), BF16),
        V((1, 1), jnp.int32),
        DMA((17,)),
        DMA,
        DMA((2,)),
        DMA,
        DMA,
        DMA((2,)),
        DMA((2,)),
        DMA,
        DMA,
        DMA((2,)),
        DMA((2,)),
        DMA,
        DMA,
    ]
    both, atom_grad = pl.pallas_call(
        functools.partial(kernel, plane, count),
        out_shape=(
            pltpu.VMEM((2 * edges, width), BF16),
            pltpu.VMEM((local, atom_width), F32),
        ),
        in_specs=[pl.BlockSpec(memory_space=pl.ANY)] * (1 + len(operands)),
        out_specs=[pl.BlockSpec(memory_space=pltpu.VMEM)] * 2,
        scratch_shapes=scratch,
        compiler_params=pltpu.CompilerParams(
            collective_id=0, has_side_effects=True, vmem_limit_bytes=VMEM
        ),
        cost_estimate=pl.CostEstimate(flops=3_000_000_000, bytes_accessed=8_000_000, transcendentals=1_000_000),
    )(trip_blocks.reshape(1, 1), *operands)
    return both[:edges], both[edges:], atom_grad


def solution(mesh):
    both = ("dp", "graph")
    rows, lanes = P(both, None), P(None, both)
    placed = (
        rows,
        P(both, None, None),
        lanes,
        rows,
        lanes,
        lanes,
        lanes,
        P(both),
        P(both),
    ) + (P(),) * 8
    return jax.shard_map(
        shards,
        mesh=mesh,
        in_specs=placed,
        out_specs=(rows, rows, rows),
        check_vma=False,
    )
```

```python
import functools

import jax
import jax.numpy as jnp
from jax import lax
from jax.experimental import pallas as pl
from jax.experimental.pallas import tpu as pltpu
from jax.sharding import PartitionSpec as P

TBLK = 256
PLANE = 8
VMEM = 56 * 1024 * 1024
F32 = jnp.float32
BF16 = jnp.bfloat16
MESH = pl.DeviceIdType.MESH


def iota(shape, dim):
    return lax.broadcasted_iota(jnp.int32, shape, dim)


def dot(left, right):
    return jnp.dot(left, right, preferred_element_type=F32)


def dot_nt(left, right):
    return lax.dot_general(left, right, (((1,), (1,)), ((), ())), preferred_element_type=F32)


def hot(mask):
    return jnp.where(mask, 1.0, 0.0).astype(BF16)


def column(row):
    count = row.shape[1]
    tall = jnp.broadcast_to(row.astype(F32), (128, count))
    return jnp.transpose(tall)


def hot_rows(row, width):
    wide = column(row).astype(jnp.int32)
    parts = [hot(wide == iota(wide.shape, 1) + start) for start in range(0, width, 128)]
    return jnp.concatenate(parts, axis=1)


def kernel(
    plane,
    count,
    *refs,
):
    n_in = 16
    blocks_hbm, *hbm = refs[: n_in + 1]
    edge_out, atom_out = refs[n_in + 1 : n_in + 3]
    vm = refs[n_in + 3 : 2 * n_in + 3]
    (
        atoms,
        fetch,
        slots_in,
        trips,
        reverse,
        angular,
        angle_w,
        radial,
        radial_w,
        down_w,
        up_ca,
        messages,
        message_w,
        source_w,
        up_ac,
        target_w,
    ) = vm
    (
        st,
        tt,
        bt,
        gate,
        pre,
        hidden,
        grad,
        down_t,
        tn,
        sn,
        rt,
        y,
        mix,
        edge_rows,
        slot_cols,
        rev_cols,
        sel,
        sel_t,
        gather_out,
        table,
        want_out,
        want_in,
        rows_out,
        rows_in,
        gather_in,
        back_out,
        back_in,
        part_out,
        part_in,
        blocks,
        in_sem,
        atom_send,
        atom_recv,
        want_send,
        want_recv,
        rows_send,
        rows_recv,
        pair_send,
        pair_recv,
        back_send,
        back_recv,
        part_send,
        part_recv,
    ) = refs[2 * n_in + 3 :]
    depth = count // plane
    half = depth // 2
    own = half // 2
    per_peer = fetch.shape[0]
    local, atom_width = atoms.shape
    share = half * per_peer
    total = plane * share
    edges, width = messages.shape
    trip_count = trips.shape[1]
    tri = down_w.shape[1]
    tile = 512

    me = lax.axis_index("graph")
    my_z, my_q = me // plane, me % plane

    def far_first(step, size):
        return size // 2 + (step // 2) * (2 * (step % 2) - 1)

    def z_peer(step):
        return (my_z + far_first(step, depth)) % depth

    def q_peer(step):
        return (my_q + far_first(step, plane)) % plane

    def to_slot(step):
        return (own + far_first(step, depth)) % depth

    def from_slot(step):
        return (own - far_first(step, depth) + depth) % depth

    def at(z, q):
        return {"graph": z * plane + q}

    def remote(src, dst, send, recv, where):
        return pltpu.make_async_remote_copy(
            src_ref=src, dst_ref=dst, send_sem=send, recv_sem=recv, device_id=where, device_id_type=MESH
        )

    def wait_recv(group, recv):
        remote(group, group, atom_send, recv, at(z_peer(1), my_q)).wait_recv()

    def wait_send(group, send):
        remote(group, group, send, atom_recv.at[0], at(z_peer(1), my_q)).wait_send()

    barrier = pltpu.get_barrier_semaphore()

    @pl.loop(1, depth)
    def _(step):
        pl.semaphore_signal(barrier, inc=1, device_id=at(z_peer(step), my_q), device_id_type=MESH)

    @pl.loop(1, plane)
    def _(step):
        pl.semaphore_signal(barrier, inc=1, device_id=at(my_z, q_peer(step)), device_id_type=MESH)

    loads = [pltpu.make_async_copy(hbm[i], vm[i], in_sem.at[i]) for i in range(n_in)]
    loads.append(pltpu.make_async_copy(blocks_hbm, blocks, in_sem.at[n_in]))
    for load in [loads[n_in]] + loads[:n_in]:
        load.start()

    loads[1].wait()
    flat = jnp.concatenate([fetch[c : c + 1, :] for c in range(per_peer)], axis=1)
    flat = jnp.broadcast_to(flat.astype(F32), (8, per_peer * count)).astype(BF16)
    from_peer = iota((per_peer * count, 128), 0)
    to_lane = iota((per_peer * count, 128), 1)
    lane_z = (my_z + (to_lane // share) * half + to_lane % half + depth - own) % depth
    lane_c = (to_lane % share) // half
    same_c = from_peer // count == lane_c
    offset = from_peer % count - lane_z * plane
    lane = iota((8, 128), 1)
    for q in range(plane):
        pick = hot(same_c & (offset == q))
        ids = dot(flat, pick).astype(jnp.int32) + (lane % half) * local
        want_out[q] = jnp.where(lane < 2 * share, ids, -1)[0:1, :]

    loads[2].wait()
    slot = slots_in[...]
    owner = slot // per_peer
    place = (owner // plane - my_z + own + depth) % depth
    slot = (place // half) * total + (owner % plane) * share + (slot % per_peer) * half + place % half
    for role in range(2):
        row = slot[role : role + 1, :]
        edge_rows[role] = hot_rows(row, 2 * total)
        slot_cols[:, role * edges : (role + 1) * edges] = hot(iota((2 * total, edges), 0) == row)

    loads[n_in].wait()
    loads[3].wait()
    live = blocks[...] * TBLK
    chunk = 512

    @pl.loop(0, trip_count // chunk)
    def _(i):
        span = pl.ds(pl.multiple_of(i * chunk, chunk), chunk)
        edge = iota((edges, chunk), 0)
        at_trip = iota((1, chunk), 1) + i * chunk
        targets = jnp.where(at_trip < live, trips[0:1, span], -1)
        tt[:, span] = hot(edge == targets)
        st[:, span] = hot(edge == trips[1:2, span])

    loads[0].wait()
    table[own] = atoms[...]

    pl.semaphore_wait(barrier, depth + plane - 2)

    def atom_copy(step, slot_at):
        return remote(atoms, table.at[slot_at], atom_send, atom_recv.at[slot_at // half], at(z_peer(step), my_q))

    @pl.loop(1, depth)
    def _(step):
        atom_copy(step, from_slot(step)).start()

    def want_copy(step, slot_at):
        return remote(
            want_out.at[q_peer(step)], want_in.at[slot_at], want_send, want_recv, at(my_z, q_peer(step))
        )

    @pl.loop(1, plane)
    def _(step):
        want_copy(step, my_q).start()

    want_in[my_q] = want_out[my_q]

    @pl.loop(0, trip_count // chunk)
    def _(i):
        span = pl.ds(pl.multiple_of(i * chunk, chunk), chunk)
        at_trip = iota((1, chunk), 1) + i * chunk
        tn[span, :] = hot_rows(jnp.where(at_trip < live, trips[0:1, span], -1), edges)
        sn[span, :] = hot_rows(trips[1:2, span], edges)

    loads[4].wait()
    rev_cols[...] = hot(iota((edges, edges), 0) == reverse[...])

    @pl.loop(0, trip_count // chunk)
    def _(i):
        span = pl.ds(pl.multiple_of(i * chunk, chunk), chunk)
        rt[:, span] = dot(rev_cols[...], tt[:, span]).astype(BF16)

    loads[5].wait()
    loads[6].wait()
    bt[...] = dot(jnp.transpose(angle_w[...].astype(F32)).astype(BF16), angular[...])
    wait_recv(want_in.at[pl.ds(0, plane - 1)], want_recv)

    for q in range(plane):
        picks = hot_rows(want_in[q], half * local)
        for part in range(2):
            sel[part, q * share : (q + 1) * share, :] = picks[part * share : (part + 1) * share]

    def rows_copy(part, step, slot_at):
        return remote(
            rows_out.at[part, q_peer(step)],
            rows_in.at[part, slot_at],
            rows_send.at[part],
            rows_recv.at[part],
            at(my_z, q_peer(step)),
        )

    def send_rows(part):
        column_rows = table[part * half : (part + 1) * half].reshape(half * local, atom_width)
        rows = dot(sel[part], column_rows).astype(BF16)
        rows_out[part] = rows.reshape(plane, share, atom_width)

        @pl.loop(1, plane)
        def _(step):
            rows_copy(part, step, my_q).start()

        rows_in[part, my_q] = rows_out[part, my_q]

    wait_recv(table.at[pl.ds(0, half - 1)], atom_recv.at[0])
    send_rows(0)

    wait_recv(table.at[pl.ds(half, half)], atom_recv.at[1])

    send_rows(1)

    for part in range(2):
        sel_t[part] = jnp.transpose(sel[part].astype(F32)).astype(BF16)
    loads[9].wait()
    down_t[...] = jnp.transpose(down_w[...].astype(F32)).astype(BF16)
    loads[11].wait()
    loads[12].wait()

    @pl.loop(0, width // tile)
    def _(i):
        span = pl.ds(pl.multiple_of(i * tile, tile), tile)
        pre[:, span] = dot(messages[...], message_w[:, span])

    loads[7].wait()
    loads[8].wait()
    gate[...] = dot(jnp.transpose(radial[...].astype(F32)).astype(BF16), radial_w[...])

    loads[10].wait()
    loads[14].wait()
    same = dot_nt(up_ca[...], up_ca[...]) + dot_nt(up_ac[...], up_ac[...])
    cross = dot_nt(up_ac[...], up_ca[...])
    cross = cross + jnp.transpose(cross)
    for part, value in enumerate((same, cross)):
        high = value.astype(BF16)
        mix[part, :tri, :] = high
        mix[part, tri:, :] = (value - high.astype(F32)).astype(BF16)
    loads[13].wait()
    loads[15].wait()

    end_rows = [None, None]
    for part in range(2):
        wait_recv(rows_in.at[part, pl.ds(0, plane - 1)], rows_recv.at[part])
        slot_rows = rows_in[part].reshape(total, atom_width)
        for role in range(2):
            found = dot(edge_rows[role, :, part * total : (part + 1) * total], slot_rows)
            end_rows[role] = found if part == 0 else end_rows[role] + found
    source_rows, target_rows = end_rows[0].astype(BF16), end_rows[1].astype(BF16)
    down = jnp.zeros((tri, edges), F32)
    for start in range(0, width, tile):
        span = slice(start, start + tile)
        part = pre[:, span] + dot(source_rows, source_w[:, span]) + dot(target_rows, target_w[:, span])
        pre[:, span] = part
        hidden[:, span] = (part * jax.nn.sigmoid(part) * gate[:, span]).astype(BF16)
        down = down + dot_nt(down_t[:, span], hidden[:, span])
    reduced = (down * jax.nn.sigmoid(down)).astype(BF16)
    terms = (dot(reduced, st[...]) * bt[...]).astype(BF16)
    gathered = dot(terms, tn[...]).astype(BF16)
    gather_out[...] = gathered

    pair_copy = remote(gather_out, gather_in, pair_send, pair_recv, at(my_z, my_q + 1 - 2 * (my_q % 2)))
    pair_copy.start()

    def mixed(part, value):
        both = dot(mix[part], value)
        return (both[:tri] + both[tri:]).astype(BF16)

    y[...] = dot(mixed(0, gathered), tt[...])
    sigma = jax.nn.sigmoid(down)
    down_slope = sigma * (1.0 + down * (1.0 - sigma))
    for start in range(0, width, tile):
        span = slice(start, start + tile)
        part = pre[:, span]
        sigma = jax.nn.sigmoid(part)
        gate[:, span] = gate[:, span] * (sigma * (1.0 + part * (1.0 - sigma)))

    pair_copy.wait_recv()

    terms = ((y[...] + dot(mixed(1, gather_in[...]), rt[...])) * bt[...]).astype(BF16)
    down_grad = dot(terms, sn[...]) * down_slope
    down_grad = jnp.transpose(down_grad).astype(BF16)
    ends = [jnp.zeros((edges, atom_width), F32) for _ in range(2)]
    for start in range(0, width, tile):
        span = slice(start, start + tile)
        part = (dot(down_grad, down_t[:, span]) * gate[:, span]).astype(BF16)
        grad[:, span] = part
        ends[0] = ends[0] + dot_nt(part, source_w[:, span])
        ends[1] = ends[1] + dot_nt(part, target_w[:, span])
    ends = jnp.concatenate([ends[0].astype(BF16), ends[1].astype(BF16)], axis=0)

    def back_copy(part, step, slot_at):
        return remote(
            back_out.at[part, q_peer(step)],
            back_in.at[part, slot_at],
            back_send.at[part],
            back_recv.at[part],
            at(my_z, q_peer(step)),
        )

    for part in (1, 0):
        back = dot(slot_cols[part * total : (part + 1) * total, :], ends).astype(BF16)
        back_out[part] = back.reshape(plane, share, atom_width)

        @pl.loop(1, plane)
        def _(step):
            back_copy(part, step, my_q).start()

        back_in[part, my_q] = back_out[part, my_q]

    mine = jnp.transpose(gather_out[...].astype(F32)).astype(BF16)
    theirs = jnp.transpose(dot(gather_in[...], rev_cols[...])).astype(BF16)
    for start in range(0, width, tile):
        span = slice(start, start + tile)
        raised = dot(mine, up_ca[:, span]) + dot(theirs, up_ac[:, span])
        edge_out[:edges, span] = raised.astype(BF16)

    def part_copy(step, slot_at):
        return remote(
            part_out.at[to_slot(step)], part_in.at[slot_at], part_send, part_recv, at(z_peer(step), my_q)
        )

    for part in (1, 0):
        wait_recv(back_in.at[part, pl.ds(0, plane - 1)], back_recv.at[part])
        sums = dot(sel_t[part], back_in[part].reshape(total, atom_width)).astype(BF16)
        part_out[part * half : (part + 1) * half] = sums.reshape(half, local, atom_width)

        @pl.loop(1 if part else half + 1, half + 1 if part else depth)
        def _(step):
            part_copy(step, from_slot(step)).start()

    part_in[own] = part_out[own]

    @pl.loop(0, width // tile)
    def _(i):
        span = pl.ds(pl.multiple_of(i * tile, tile), tile)
        edge_out[edges:, span] = dot_nt(grad[...], message_w[span, :]).astype(BF16)

    wait_recv(part_in.at[pl.ds(0, depth - 1)], part_recv)

    owned = part_in[0].astype(F32)
    for z in range(1, depth):
        owned = owned + part_in[z].astype(F32)
    atom_out[...] = owned

    wait_send(table.at[pl.ds(0, depth - 1)], atom_send)
    wait_send(want_out.at[pl.ds(0, plane - 1)], want_send)
    for part in range(2):
        wait_send(rows_out.at[part, pl.ds(0, plane - 1)], rows_send.at[part])
        wait_send(back_out.at[part, pl.ds(0, plane - 1)], back_send.at[part])
    wait_send(part_out.at[pl.ds(0, depth - 1)], part_send)
    pair_copy.wait_send()


def shards(
    atoms,
    fetch_rows,
    edge_slots,
    messages,
    radial,
    angular,
    trip_edges,
    trip_blocks,
    reverse_slot,
    message_weight,
    source_weight,
    target_weight,
    radial_weight,
    down_weight,
    angle_weight,
    up_ca_weight,
    up_ac_weight,
):
    count = lax.axis_size("graph")
    plane = PLANE
    depth = count // plane
    local, atom_width = atoms.shape
    edges, width = messages.shape
    tri = down_weight.shape[1]
    trip_count = trip_edges.shape[1]
    per_peer = fetch_rows.shape[2]
    half = depth // 2
    share = half * per_peer
    total = plane * share
    fetch = jnp.transpose(fetch_rows[0])
    operands = (
        atoms,
        fetch,
        edge_slots,
        trip_edges,
        reverse_slot.reshape(1, edges),
        angular,
        angle_weight,
        radial,
        radial_weight,
        down_weight,
        up_ca_weight,
        messages,
        message_weight,
        source_weight,
        up_ac_weight,
        target_weight,
    )
    V = pltpu.VMEM
    DMA = pltpu.SemaphoreType.DMA
    scratch = [V(x.shape, x.dtype) for x in operands] + [
        V((edges, trip_count), BF16),
        V((edges, trip_count), BF16),
        V((tri, trip_count), F32),
        V((edges, width), F32),
        V((edges, width), F32),
        V((edges, width), BF16),
        V((edges, width), BF16),
        V((tri, width), BF16),
        V((trip_count, edges), BF16),
        V((trip_count, edges), BF16),
        V((edges, trip_count), BF16),
        V((tri, trip_count), F32),
        V((2, 2 * tri, tri), BF16),
        V((2, edges, 2 * total), BF16),
        V((2 * total, 2 * edges), BF16),
        V((edges, edges), BF16),
        V((2, total, half * local), BF16),
        V((2, half * local, total), BF16),
        V((tri, edges), BF16),
        V((depth, local, atom_width), BF16),
        V((plane, 1, 128), jnp.int32),
        V((plane, 1, 128), jnp.int32),
        V((2, plane, share, atom_width), BF16),
        V((2, plane, share, atom_width), BF16),
        V((tri, edges), BF16),
        V((2, plane, share, atom_width), BF16),
        V((2, plane, share, atom_width), BF16),
        V((depth, local, atom_width), BF16),
        V((depth, local, atom_width), BF16),
        V((1, 1), jnp.int32),
        DMA((17,)),
        DMA,
        DMA((2,)),
        DMA,
        DMA,
        DMA((2,)),
        DMA((2,)),
        DMA,
        DMA,
        DMA((2,)),
        DMA((2,)),
        DMA,
        DMA,
    ]
    both, atom_grad = pl.pallas_call(
        functools.partial(kernel, plane, count),
        out_shape=(
            pltpu.VMEM((2 * edges, width), BF16),
            pltpu.VMEM((local, atom_width), F32),
        ),
        in_specs=[pl.BlockSpec(memory_space=pl.ANY)] * (1 + len(operands)),
        out_specs=[pl.BlockSpec(memory_space=pltpu.VMEM)] * 2,
        scratch_shapes=scratch,
        compiler_params=pltpu.CompilerParams(
            collective_id=0, has_side_effects=True, vmem_limit_bytes=VMEM
        ),
        cost_estimate=pl.CostEstimate(flops=3_000_000_000, bytes_accessed=8_000_000, transcendentals=1_000_000),
    )(trip_blocks.reshape(1, 1), *operands)
    return both[:edges], both[edges:], atom_grad


def solution(mesh):
    both = ("dp", "graph")
    rows, lanes = P(both, None), P(None, both)
    placed = (
        rows,
        P(both, None, None),
        lanes,
        rows,
        lanes,
        lanes,
        lanes,
        P(both),
        P(both),
    ) + (P(),) * 8
    return jax.shard_map(
        shards,
        mesh=mesh,
        in_specs=placed,
        out_specs=(rows, rows, rows),
        check_vma=False,
    )
```
